128 devices in a mesh: dp: 16 (over x, z_lo, core), mp: 8 (over z_hi, y).
Axes of the slice: x: 4, y: 4, z: 4 (z_hi: 2, z_lo: 2; z = z_hi * 2 + z_lo), core: 2. Of those that a mesh axis runs over, the one named last changes fastest.
Arguments:
- taps: bfloat16 [3, 512, 8192], P(None, ('dp', 'mp')), may hold values from -6 to 6
- gain: float32 [8192], P('dp'), may hold values from 0.5 to 1.5
- join_weight: bfloat16 [3, 8192, 8192], P(None, 'mp', 'dp'), may hold values from -0.0390625 to 0.0390625
- head_weight: bfloat16 [8192, 16384], P('mp', 'dp'), may hold values from -0.1875 to 0.1875
- targets: int32 [2, 16, 32], P(None, None, 'mp'), may hold values from 0 to 16383
- masks: int32 [2, 16, 32], P(None, None, 'mp'), may hold values from 0 to 1, as said below
- first_codes: bfloat16 [3, 8192, 8192], P(None, 'mp', 'dp'), may hold values from -1 to 1
- first_scales: float32 [3, 8192, 32], P(None, 'mp', 'dp'), may hold values from 1e-05 to 0.0001
- second_codes: bfloat16 [3, 8192, 8192], P(None, 'mp', 'dp'), may hold values from 0.099609375 to 1
- second_scales: float32 [3, 8192, 32], P(None, 'mp', 'dp'), may hold values from 1e-10 to 1e-09
Outputs:
- new_join: bfloat16 [3, 8192, 8192], P(None, 'mp', 'dp')
- new_first_codes: bfloat16 [3, 8192, 8192], P(None, 'mp', 'dp')
- new_first_scales: float32 [3, 8192, 32], P(None, 'mp', 'dp')
- new_second_codes: bfloat16 [3, 8192, 8192], P(None, 'mp', 'dp')
- new_second_scales: float32 [3, 8192, 32], P(None, 'mp', 'dp')
- loss: float32 [], replicated
The draws below stay inside these ranges and needn't reach their ends.
Inputs may be any that keep to these rules, and one draw needn't show every extreme that they name: Every step k has at least one token with masks[k] = 1.
All inputs are finite; a program needn't handle non-finite values. Where the reference program divides by a largest or mean magnitude, that divisor is 1e-20 or more.
Results may differ from the reference program's by a relative error of at most 0.01.
Values may be sent and summed in bfloat16 or wider, within the bound.
No kernel may reach another device: no remote copies, remote signals or barrier semaphores. Data moves between devices by JAX's collectives and lax.ppermute only.
A program may use at most 128 MiB of HBM per device.

```python
import math
import jax
import jax.numpy as jnp
from jax import lax

D = 8192
V = 16384
TOK_DEV = 32
STEPS = 2
BLOCK = 256
TOKENS = 512
GROUPS = 16


def draw_masks(key, part):
    key = jax.random.fold_in(key, 7)
    key_votes, key_pick = jax.random.split(key)
    mask_shape = (STEPS, GROUPS, TOK_DEV)
    ballots = jax.random.randint(key_votes, mask_shape, 0, 10 * TOK_DEV)
    positions = lax.broadcasted_iota(jnp.int32, mask_shape, 2)
    group_ids = lax.broadcasted_iota(jnp.int32, mask_shape, 1)
    is_live = ballots < 2 * TOK_DEV + 6 * positions
    flat_index = group_ids * TOK_DEV + positions
    chosen_slot = jax.random.randint(key_pick, (STEPS, 1, 1), 0, GROUPS * TOK_DEV)
    return jnp.where(is_live | (flat_index == chosen_slot), 1, 0).astype(jnp.int32)


def plant(result, rng, least, top_value):
    longest = result.shape.index(max(result.shape))
    spots = []
    for shift in (0, 1):
        where = [jax.random.randint(jax.random.fold_in(rng, axis), (), 0, length) for axis, length in enumerate(result.shape)]
        where[longest] = (where[longest] + shift) % result.shape[longest]
        spots.append(tuple(where))
    return result.at[spots[0]].set(least).at[spots[1]].set(top_value)


def block_scale(key, dims, pieces, low, top_value):
    def one(axis_at, parts):
        steps = jax.random.uniform(jax.random.fold_in(jax.random.fold_in(key, 6), axis_at), (parts,), jnp.float32, low / len(pieces), top_value / len(pieces))
        return jnp.repeat(jnp.exp(steps), dims[axis_at] // parts).reshape((-1,) + (1,) * (len(dims) - axis_at - 1))

    loudness = one(*pieces[0])
    for cut in pieces[1:]:
        loudness = loudness * one(*cut)
    return loudness


def bell_draw(own_key, extent, spread, bound, pieces=(), dtype=jnp.bfloat16):
    loudness = block_scale(own_key, extent, pieces, -0.22, 0.18) if pieces else 1.0
    entries = jax.random.normal(own_key, extent, jnp.float32) * spread * loudness
    return jnp.minimum(jnp.maximum(entries, -bound), bound).astype(dtype)


def setup_inputs(seed: int = 0) -> dict:
    keys = jax.random.split(jax.random.key(seed), 11)
    return {
        "taps": bell_draw(keys[0], (3, TOKENS, D), 1.0, 6.0, ((1, 128),)),
        "gain": jnp.clip(1.0 + 0.1 * jax.random.normal(keys[1], (D,), jnp.float32), 0.5, 1.5),
        "join_weight": bell_draw(keys[2], (3, D, D), (3 * D) ** -0.5, 0.0390625, ((1, 8), (2, 16))),
        "head_weight": bell_draw(keys[3], (D, V), (D // 9) ** -0.5, 0.1875, ((0, 8), (1, 16))),
        "targets": plant(jax.random.randint(keys[4], (STEPS, GROUPS, TOK_DEV), 0, V), jax.random.fold_in(keys[4], 1), 0, V - 1).astype(jnp.int32),
        "masks": draw_masks(jax.random.fold_in(keys[10], 71), 0),
        "first_codes": jnp.clip(jax.random.uniform(keys[6], (3, D, D), jnp.float32, -1.0, 1.0) * block_scale(keys[6], (3, D, D), ((1, 8), (2, 16)), -0.4, 0.0), -1.0, 1.0).astype(jnp.bfloat16),
        "first_scales": jnp.clip(jnp.exp(math.log(0.0001) - 2.3025851 * jax.random.uniform(keys[7], (3, D, D // BLOCK), jnp.float32) ** block_scale(keys[7], (3, D, D // BLOCK), ((1, 8), (2, 16)), -0.2, 0.2)), 9.999999747378752e-06, 0.0001),
        "second_codes": jnp.clip(0.099609375 + 0.9003906 * jax.random.uniform(keys[8], (3, D, D), jnp.float32) ** block_scale(keys[8], (3, D, D), ((1, 8), (2, 16)), -0.2, 0.2), 0.099609375, 1.0).astype(jnp.bfloat16),
        "second_scales": jnp.clip(jnp.exp(math.log(9.999999717180685e-10) - 2.3025851 * jax.random.uniform(keys[9], (3, D, D // BLOCK), jnp.float32) ** block_scale(keys[9], (3, D, D // BLOCK), ((1, 8), (2, 16)), -0.2, 0.2)), 1.000000013351432e-10, 9.999999717180685e-10),
    }


norm_eps = 1e-05
clip_norm = 1.0
learn_rate = 0.0003
weight_decay = 0.1
beta_first = 0.9
beta_second = 0.999
step_count = 10.0
adam_eps = 1e-08
scale_eps = 1e-12

def contract_first(left, right):
    return lax.dot_general(left, right, (((0,), (0,)), ((), ())), preferred_element_type=jnp.float32)

def contract_last(left, right):
    return lax.dot_general(left, right, (((1,), (1,)), ((), ())), preferred_element_type=jnp.float32)

def adam_blocks(weights, grads, first_codes, first_scales, second_codes, second_scales):
    shape = weights.shape
    blocked = shape[:-1] + (shape[-1] // BLOCK, BLOCK)
    grad_blocks = grads.reshape(blocked)
    first_prev = first_codes.astype(jnp.float32).reshape(blocked) * first_scales[..., None]
    second_prev = second_codes.astype(jnp.float32).reshape(blocked) * second_scales[..., None]
    first_new = beta_first * first_prev + (1.0 - beta_first) * grad_blocks
    second_new = beta_second * second_prev + (1.0 - beta_second) * grad_blocks * grad_blocks
    current = weights.astype(jnp.float32).reshape(blocked)
    update = first_new / (1.0 - beta_first ** step_count) / (jnp.sqrt(second_new / (1.0 - beta_second ** step_count)) + adam_eps) + weight_decay * current
    new_weights = (current - learn_rate * update).reshape(shape).astype(jnp.bfloat16)
    first_scale = lax.optimization_barrier(jnp.max(jnp.abs(first_new), -1)) + scale_eps
    first_out = (first_new / first_scale[..., None]).reshape(shape).astype(jnp.bfloat16)
    second_scale = lax.optimization_barrier(jnp.max(jnp.abs(second_new), -1)) + scale_eps
    second_out = (second_new / second_scale[..., None]).reshape(shape).astype(jnp.bfloat16)
    return (new_weights, first_out, first_scale, second_out, second_scale)

def reference(taps, gain, join_weight, head_weight, targets, masks, first_codes, first_scales, second_codes, second_scales):
    target_ids = targets.reshape(STEPS, TOKENS)
    mask_float = masks.reshape(STEPS, TOKENS).astype(jnp.float32)
    counts = lax.optimization_barrier(jnp.sum(mask_float, 1))
    constant = jnp.dot(taps[0], join_weight[0], preferred_element_type=jnp.float32) + jnp.dot(taps[1], join_weight[1], preferred_element_type=jnp.float32)
    vocab_ids = lax.broadcasted_iota(jnp.int32, (TOKENS, V), 1)
    top_rows = taps[2]
    saved = []
    loss = jnp.zeros((), jnp.float32)
    for step in range(STEPS):
        joining = constant + jnp.dot(top_rows, join_weight[2], preferred_element_type=jnp.float32)
        inverse = lax.rsqrt(lax.optimization_barrier(jnp.sum(joining * joining, -1)) / D + norm_eps)
        hidden = (joining * inverse[:, None] * gain).astype(jnp.bfloat16)
        logits = jnp.dot(hidden, head_weight, preferred_element_type=jnp.float32)
        onehot = (vocab_ids == target_ids[step][:, None]).astype(jnp.float32)
        log_total = jnp.log(lax.optimization_barrier(jnp.sum(jnp.exp(logits), -1)))
        picked = lax.optimization_barrier(jnp.sum(logits * onehot, -1))
        loss = loss + jnp.sum(mask_float[step] * (log_total - picked) / counts[step])
        probs = jnp.exp(logits - log_total[:, None])
        logit_grad = ((mask_float[step] / counts[step])[:, None] * (probs - onehot)).astype(jnp.bfloat16)
        saved.append((top_rows, joining, inverse, logit_grad))
        top_rows = hidden
    grads = jnp.zeros(join_weight.shape, jnp.float32)
    later_grad = None
    for step in reversed(range(STEPS)):
        top_rows, joining, inverse, logit_grad = saved[step]
        hidden_grad = contract_last(logit_grad, head_weight)
        if later_grad is not None:
            hidden_grad = hidden_grad + contract_last(later_grad, join_weight[2])
        scaled = hidden_grad * gain
        inner = lax.optimization_barrier(jnp.sum(scaled * joining, -1))
        joining_grad = (inverse[:, None] * scaled - (inverse * inverse * inverse * inner / D)[:, None] * joining).astype(jnp.bfloat16)
        grads = grads + jnp.stack([contract_first(taps[0], joining_grad), contract_first(taps[1], joining_grad), contract_first(top_rows, joining_grad)])
        later_grad = joining_grad
    norm_sq = jnp.sum(grads * grads)
    clip = jnp.minimum(1.0, clip_norm / (jnp.sqrt(norm_sq) + 1e-06))
    new_join, new_first, first_scale, new_second, second_scale = adam_blocks(join_weight, grads * clip, first_codes, first_scales, second_codes, second_scales)
    return (new_join, new_first, first_scale, new_second, second_scale, loss)
```

```python
import jax
import jax.numpy as jnp
from jax import lax
from jax.experimental import pallas as pl
from jax.experimental.pallas import tpu as pltpu
from jax.sharding import Mesh, PartitionSpec as P

D = 8192
STEPS = 2
BLOCK = 256
LANES = 128

norm_eps = 1e-05
clip_norm = 1.0
learn_rate = 0.0003
weight_decay = 0.1
beta_first = 0.9
beta_second = 0.999
step_count = 10.0
adam_eps = 1e-08
scale_eps = 1e-12

bf16 = jnp.bfloat16
f32 = jnp.float32
AXES = ("p", "b", "m")
VMEM = pl.BlockSpec(memory_space=pltpu.VMEM)
SMEM = pl.BlockSpec(memory_space=pltpu.SMEM)


def dot(left, right):
    return jnp.dot(left, right, preferred_element_type=f32)


def contract_last(left, right):
    return lax.dot_general(
        left, right, (((1,), (1,)), ((), ())), preferred_element_type=f32
    )


def contract_first(left, right):
    return lax.dot_general(
        left, right, (((0,), (0,)), ((), ())), preferred_element_type=f32
    )


def halves(value):
    high = lax.reduce_precision(value, 8, 7)
    return high.astype(bf16), (value - high).astype(bf16)


def side_lanes(*columns):
    shape = columns[0].shape[:-1] + (LANES,)
    lane = lax.broadcasted_iota(jnp.int32, shape, len(shape) - 1)
    block = jnp.zeros(shape, bf16)
    for place, column in enumerate(columns):
        block = jnp.where(lane == place, column, block)
    return block


def read_lanes(block, first, last):
    wide = block.astype(f32)
    lane = lax.broadcasted_iota(jnp.int32, wide.shape, wide.ndim - 1)
    inside = (lane >= first) & (lane <= last)
    return jnp.sum(jnp.where(inside, wide, 0.0), -1, keepdims=True)


def half_out_kernel(core, taps, out):
    sets, _, width = taps.shape
    chunks = width // 1024
    other = (1 - core[0]) * 512
    for s in range(sets):
        for chunk in range(chunks):
            start = pl.multiple_of(chunk * 1024 + other, 512)
            out[s, :, chunk * 512 : (chunk + 1) * 512] = taps[s, :, pl.ds(start, 512)]


def half_join_kernel(core, taps, received, out):
    sets, _, width = taps.shape
    chunks = width // 1024
    copies = out.shape[0] // chunks
    own = core[0] * 512
    first = core[0] == 0
    for chunk in range(chunks):
        rows = []
        for s in range(sets):
            start = pl.multiple_of(chunk * 1024 + own, 512)
            mine = taps[s, :, pl.ds(start, 512)].astype(f32)
            theirs = received[s, :, chunk * 512 : (chunk + 1) * 512].astype(f32)
            rows.append(jnp.where(first, mine, theirs))
            rows.append(jnp.where(first, theirs, mine))
        block = jnp.concatenate(rows, axis=0).astype(bf16)
        for copy in range(copies):
            out[chunk * copies + copy] = block


def grad_kernel(core, left, left_later, right, right_later, grad, squares):
    value = contract_first(left[0, 0], right[0]) + contract_first(
        left_later[0, 0], right_later[0]
    )
    grad[0] = value
    total = jnp.sum((value * value).reshape(-1, 8, 512), 0)
    folded = total[:, :128] + total[:, 128:256] + total[:, 256:384] + total[:, 384:]
    start = (pl.program_id(0) == 0) & (pl.program_id(1) == 0)

    @pl.when(start)
    def _():
        squares[...] = folded

    @pl.when(jnp.logical_not(start))
    def _():
        squares[...] += folded


def gradients(core, left, right):
    tokens = left.shape[2]

    def left_block(s, h, core):
        return (h ^ core[0], s, 0, 0)

    def left_later_block(s, h, core):
        return (h ^ core[0], jnp.where(s == 2, 3, s), 0, 0)

    return pl.pallas_call(
        grad_kernel,
        grid_spec=pltpu.PrefetchScalarGridSpec(
            num_scalar_prefetch=1,
            grid=(3, 2),
            in_specs=[
                pl.BlockSpec((1, 1, tokens, 512), left_block),
                pl.BlockSpec((1, 1, tokens, 512), left_later_block),
                pl.BlockSpec((1, tokens, 512), lambda s, h, core: (0, 0, 0)),
                pl.BlockSpec(
                    (1, tokens, 512), lambda s, h, core: (jnp.where(s == 2, 2, 1), 0, 0)
                ),
            ],
            out_specs=[
                pl.BlockSpec((1, 512, 512), lambda s, h, core: (s, h, 0)),
                pl.BlockSpec((8, 128), lambda s, h, core: (0, 0)),
            ],
        ),
        out_shape=[
            jax.ShapeDtypeStruct((3, 1024, 512), f32),
            jax.ShapeDtypeStruct((8, 128), f32),
        ],
        compiler_params=pltpu.CompilerParams(vmem_limit_bytes=40 * 2**20),
        cost_estimate=pl.CostEstimate(
            flops=6 * 4 * 512 * 512 * 512, bytes_accessed=10 * 2**20, transcendentals=0
        ),
        name="gradients",
    )(core, left, left, right, right)


def adam_kernel(
    clip, weight, grad, first, second, first_scale, second_scale,
    new_weight, new_first, new_second, new_first_scale, new_second_scale,
):
    rows = weight.shape[1]
    clip_value = clip[0]
    old_scales = jnp.concatenate(
        [first_scale[0], second_scale[0], jnp.zeros((4, rows), f32)], axis=0
    ).T
    new_columns = []
    for block in range(2):
        span = slice(block * BLOCK, (block + 1) * BLOCK)
        clipped = grad[0, :, span] * clip_value
        first_new = (
            first[0, :, span].astype(f32) * (beta_first * old_scales[:, block : block + 1])
            + (1.0 - beta_first) * clipped
        )
        second_new = (
            second[0, :, span].astype(f32)
            * (beta_second * old_scales[:, 2 + block : 3 + block])
            + (1.0 - beta_second) * clipped * clipped
        )
        current = weight[0, :, span].astype(f32)
        update = (
            first_new
            * (1.0 / (1.0 - beta_first**step_count))
            / (jnp.sqrt(second_new * (1.0 / (1.0 - beta_second**step_count))) + adam_eps)
            + weight_decay * current
        )
        new_weight[0, :, span] = (current - learn_rate * update).astype(bf16)
        first_top = jnp.max(jnp.abs(first_new), -1, keepdims=True) + scale_eps
        second_top = jnp.max(jnp.abs(second_new), -1, keepdims=True) + scale_eps
        new_first[0, :, span] = (first_new * (1.0 / first_top)).astype(bf16)
        new_second[0, :, span] = (second_new * (1.0 / second_top)).astype(bf16)
        new_columns.append((first_top, second_top))
    lane = lax.broadcasted_iota(jnp.int32, (rows, LANES), 1)
    table = jnp.zeros((rows, LANES), f32)
    for block, (first_top, second_top) in enumerate(new_columns):
        table = jnp.where(lane == block, first_top, table)
        table = jnp.where(lane == 2 + block, second_top, table)
    turned = table.T
    new_first_scale[0] = turned[0:2]
    new_second_scale[0] = turned[2:4]


def adam(clip, weight, grad, first, second, first_scale, second_scale):
    rows = 256
    wide = pl.BlockSpec((1, rows, 512), lambda s, i: (s, i, 0))
    thin = pl.BlockSpec((1, 2, rows), lambda s, i: (s, 0, i))
    return pl.pallas_call(
        adam_kernel,
        grid=(3, 1024 // rows),
        in_specs=[SMEM, wide, wide, wide, wide, thin, thin],
        out_specs=[wide, wide, wide, thin, thin],
        out_shape=[
            jax.ShapeDtypeStruct((3, 1024, 512), bf16),
            jax.ShapeDtypeStruct((3, 1024, 512), bf16),
            jax.ShapeDtypeStruct((3, 1024, 512), bf16),
            jax.ShapeDtypeStruct((3, 2, 1024), f32),
            jax.ShapeDtypeStruct((3, 2, 1024), f32),
        ],
        compiler_params=pltpu.CompilerParams(vmem_limit_bytes=40 * 2**20),
        name="update",
    )(clip, weight, grad, first, second, first_scale, second_scale)


def shards(
    taps, gain, join_weight, head_weight, targets, masks,
    first_codes, first_scales, second_codes, second_scales,
):
    row_count = lax.axis_size("p")
    column_count = lax.axis_size("m")
    core_count = lax.axis_size("b")
    core = lax.axis_index("b")
    core_array = core.reshape(1).astype(jnp.int32)
    turn_pairs = [
        ((p * core_count + b) * column_count + m, (m * core_count + b) * column_count + p)
        for p in range(row_count)
        for b in range(core_count)
        for m in range(column_count)
    ]

    def turn(value):
        return lax.ppermute(value, AXES, turn_pairs)

    def swap(value):
        return lax.ppermute(value, "b", [(0, 1), (1, 0)])

    def exchange(value, axis):
        return lax.all_to_all(value, axis, 0, 0, tiled=False)

    def spread(value, axis):
        copies = lax.axis_size(axis)
        return exchange(jnp.broadcast_to(value, (copies,) + value.shape), axis)

    def own_rows(weight):
        return lax.dynamic_slice_in_dim(weight, core * 512, 512, weight.ndim - 2)

    def other_rows(weight):
        return lax.dynamic_slice_in_dim(weight, (1 - core) * 512, 512, weight.ndim - 2)

    join_own, join_other = own_rows(join_weight), other_rows(join_weight)
    head_own, head_other = own_rows(head_weight), other_rows(head_weight)
    target_ids = targets.reshape(STEPS, 64, 1)
    mask_float = masks.astype(f32).reshape(STEPS, 64, 1)
    live = jnp.sum(mask_float, axis=1, keepdims=True)
    gain_row = gain.reshape(1, 512)

    with jax.named_scope("taps_in"):
        outgoing = pl.pallas_call(
            half_out_kernel,
            in_specs=[SMEM, VMEM],
            out_specs=VMEM,
            out_shape=jax.ShapeDtypeStruct((3, 4, D // 2), bf16),
            name="half_out",
        )(core_array, taps)
        incoming = swap(outgoing)
        packed = pl.pallas_call(
            half_join_kernel,
            in_specs=[SMEM, VMEM, VMEM],
            out_specs=VMEM,
            out_shape=jax.ShapeDtypeStruct((64, 24, 512), bf16),
            compiler_params=pltpu.CompilerParams(vmem_limit_bytes=24 * 2**20),
            name="half_join",
        )(core_array, taps, incoming)
        landed = exchange(packed, ("m", "p"))
        taps_own = landed.reshape(64, 3, 8, 512).transpose(1, 0, 2, 3).reshape(3, 512, 512)
        taps_other = swap(taps_own)

    with jax.named_scope("join_first"):
        constant_part = (
            dot(taps_own[0], join_own[0])
            + dot(taps_own[1], join_own[1])
            + dot(taps_other[0], join_other[0])
            + dot(taps_other[1], join_other[1])
        )
        top_part = dot(taps_own[2], join_own[2]) + dot(taps_other[2], join_other[2])
        parts = jnp.concatenate(
            [constant_part.astype(bf16), top_part.astype(bf16)], axis=1
        ).reshape(8, 64, 1024)
        sums = jnp.sum(exchange(parts, "m").astype(f32), 0)
        constant = sums[:, :512]
        joining_first = constant + sums[:, 512:]

    def to_columns(joining):
        squares = jnp.sum(joining * joining, -1, keepdims=True)
        payload = jnp.concatenate(
            [(joining * gain_row).astype(bf16), side_lanes(*halves(squares))], axis=1
        )
        mine = spread(turn(payload), "p").reshape(512, 640)
        theirs = swap(mine)
        both = read_lanes(mine[:, 512:], 0, 1) + read_lanes(theirs[:, 512:], 0, 1)
        return mine[:, :512], theirs[:, :512], both

    with jax.named_scope("hidden_first"):
        hidden_own, hidden_other, squares_first = to_columns(joining_first)

    with jax.named_scope("join_second"):
        part = dot(hidden_own, join_own[2]) + dot(hidden_other, join_other[2])
        live_rows = jnp.broadcast_to(live, (STEPS, 512, 1)).astype(bf16)
        payload = jnp.concatenate(
            [part.astype(bf16), side_lanes(*halves(squares_first), live_rows[0], live_rows[1])],
            axis=1,
        )
        got = exchange(payload.reshape(8, 64, 640), "m")
        sums = jnp.sum(got.astype(f32), 0)
        inverse_first = lax.rsqrt(read_lanes(sums[:, 512:], 0, 1) / D + norm_eps)
        counts = [read_lanes(sums[:, 512:], 2, 2), read_lanes(sums[:, 512:], 3, 3)]
        fed_back = inverse_first * sums[:, :512]
        joining_second = constant + fed_back
        logit_part_first = dot(hidden_own, head_own) + dot(hidden_other, head_other)

    with jax.named_scope("hidden_second"):
        later_own, later_other, squares_second = to_columns(joining_second)

    with jax.named_scope("logits"):
        logit_part_second = dot(later_own, head_own) + dot(later_other, head_other)
        payload = jnp.concatenate(
            [
                logit_part_second.astype(bf16),
                logit_part_first.astype(bf16),
                side_lanes(*halves(squares_second)),
            ],
            axis=1,
        )
        got = exchange(payload.reshape(8, 64, 2176), "m")
        sums = jnp.sum(got.astype(f32), 0)
        inverse_second = lax.rsqrt(read_lanes(sums[:, 2048:], 0, 1) / D + norm_eps)
        logits = [inverse_first * sums[:, 1024:2048], inverse_second * sums[:, :1024]]

    with jax.named_scope("softmax"):
        vocab = lax.broadcasted_iota(jnp.int32, (64, 1024), 1) + (
            lax.axis_index("p") * core_count + core
        ) * 1024
        hits = [vocab == target_ids[k] for k in range(STEPS)]
        stats = []
        for k in range(STEPS):
            top = jnp.max(logits[k], -1)
            weights = jnp.exp(logits[k] - top[:, None])
            stats += [
                top,
                jnp.sum(weights, -1),
                jnp.sum(weights * logits[k], -1),
                jnp.sum(jnp.where(hits[k], logits[k], 0.0), -1),
            ]
        shared = spread(jnp.stack(stats), ("p", "b"))
        loss_local = jnp.zeros((1, 1), f32)
        grad_rows, turns = [], []
        for k in range(STEPS):
            tops = shared[:, 4 * k]
            top = jnp.max(tops, 0)
            factor = jnp.exp(tops - top)
            total = jnp.sum(shared[:, 4 * k + 1] * factor, 0)
            mean = jnp.sum(shared[:, 4 * k + 2] * factor, 0) / total
            picked = jnp.sum(shared[:, 4 * k + 3], 0)
            log_total = top + jnp.log(total)
            columns = jnp.stack([log_total, log_total - picked, mean - picked], 1)
            token_weight = mask_float[k] / counts[k]
            loss_local += jnp.sum(token_weight * columns[:, 1:2], 0, keepdims=True)
            turns.append(token_weight * columns[:, 2:3])
            probs = jnp.exp(logits[k] - columns[:, 0:1])
            grad_rows.append(
                (token_weight * (probs - hits[k].astype(f32))).astype(bf16)
            )

    with jax.named_scope("logit_grads"):
        all_grads = spread(jnp.concatenate(grad_rows, 1), "m").reshape(512, 2048)
        grads_first, grads_second = all_grads[:, :1024], all_grads[:, 1024:]

    with jax.named_scope("back_second"):
        away = swap(contract_last(grads_second, head_other).astype(bf16))
        kept = contract_last(grads_second, head_own) + away.astype(f32)
        landed = exchange(kept.astype(bf16).reshape(8, 64, 512), "p")
        row_grad = turn(jnp.sum(landed.astype(f32), 0).astype(bf16)).astype(f32)
        back_second = (
            inverse_second * gain_row * row_grad
            - (inverse_second * inverse_second * turns[1] / D) * joining_second
        ).astype(bf16)
        inner = jnp.sum(back_second.astype(f32) * fed_back, -1, keepdims=True)
        loss_rows = jnp.broadcast_to(loss_local, (64, 1))
        payload = jnp.concatenate(
            [back_second, side_lanes(*halves(inner), *halves(inverse_first), *halves(loss_rows))],
            axis=1,
        )
        got = spread(payload, "m")
        loss = jnp.sum(read_lanes(got[:, 0, 512:], 4, 5))
        got = got.reshape(512, 640)
        second_all = got[:, :512]
        inner_all = read_lanes(got[:, 512:], 0, 1)
        second_scaled = (
            second_all.astype(f32) * read_lanes(got[:, 512:], 2, 3)
        ).astype(bf16)

    with jax.named_scope("back_first"):
        away = contract_last(second_all, join_other[2]) + contract_last(grads_first, head_other)
        away = swap(
            jnp.concatenate([away.astype(bf16), side_lanes(*halves(inner_all))], axis=1)
        )
        kept = (
            contract_last(second_all, join_own[2])
            + contract_last(grads_first, head_own)
            + away[:, :512].astype(f32)
        )
        inner_chip = inner_all + read_lanes(away[:, 512:], 0, 1)
        payload = jnp.concatenate([kept.astype(bf16), side_lanes(*halves(inner_chip))], axis=1)
        landed = jnp.sum(exchange(payload.reshape(8, 64, 640), "p").astype(f32), 0)
        payload = jnp.concatenate(
            [
                landed[:, :512].astype(bf16),
                side_lanes(*halves(read_lanes(landed[:, 512:], 0, 1))),
            ],
            axis=1,
        )
        row_grad = turn(payload)
        inner = turns[0] + read_lanes(row_grad[:, 512:], 0, 1)
        back_first = (
            inverse_first * gain_row * row_grad[:, :512].astype(f32)
            - (inverse_first * inverse_first * inner / D) * joining_first
        ).astype(bf16)
        first_all = spread(back_first, "m").reshape(512, 512)

    with jax.named_scope("gradients"):
        left = jnp.stack(
            [
                jnp.concatenate([taps_own, hidden_own[None]], 0),
                jnp.concatenate([taps_other, hidden_other[None]], 0),
            ]
        )
        right = jnp.stack([first_all, second_all, second_scaled])
        grads, squares = gradients(core_array, left, right)
        square_sum = jnp.broadcast_to(jnp.sum(squares), (1, LANES))
        norm_sq = jnp.sum(spread(square_sum, AXES)[:, 0, 0])
        clip = jnp.minimum(1.0, clip_norm / (jnp.sqrt(norm_sq) + 1e-06))

    with jax.named_scope("update"):
        new_join, new_first, new_second, first_scale, second_scale = adam(
            clip.reshape(1),
            join_weight,
            grads,
            first_codes,
            second_codes,
            jnp.swapaxes(first_scales, 1, 2),
            jnp.swapaxes(second_scales, 1, 2),
        )
    return (
        new_join,
        new_first,
        jnp.swapaxes(first_scale, 1, 2),
        new_second,
        jnp.swapaxes(second_scale, 1, 2),
        loss,
    )


def solution(mesh):
    rows = mesh.shape["dp"] // 2
    fine = Mesh(mesh.devices.reshape(rows, 2, mesh.shape["mp"]), AXES)
    dp, mp = ("p", "b"), "m"
    return jax.shard_map(
        shards,
        mesh=fine,
        in_specs=(
            P(None, ("p", "b", "m"), None),
            P(dp),
            P(None, mp, dp),
            P(mp, dp),
            P(None, None, mp),
            P(None, None, mp),
            P(None, mp, dp),
            P(None, mp, dp),
            P(None, mp, dp),
            P(None, mp, dp),
        ),
        out_specs=(
            P(None, mp, dp),
            P(None, mp, dp),
            P(None, mp, dp),
            P(None, mp, dp),
            P(None, mp, dp),
            P(),
        ),
        check_vma=False,
    )
```

```python
import jax
import jax.numpy as jnp
from jax import lax
from jax.experimental import pallas as pl
from jax.experimental.pallas import tpu as pltpu
from jax.sharding import Mesh, PartitionSpec as P

D = 8192
STEPS = 2
BLOCK = 256
LANES = 128

norm_eps = 1e-05
clip_norm = 1.0
learn_rate = 0.0003
weight_decay = 0.1
beta_first = 0.9
beta_second = 0.999
step_count = 10.0
adam_eps = 1e-08
scale_eps = 1e-12

bf16 = jnp.bfloat16
f32 = jnp.float32
AXES = ("p", "b", "m")
VMEM = pl.BlockSpec(memory_space=pltpu.VMEM)
SMEM = pl.BlockSpec(memory_space=pltpu.SMEM)


def dot(left, right):
    return jnp.dot(left, right, preferred_element_type=f32)


def contract_last(left, right):
    return lax.dot_general(
        left, right, (((1,), (1,)), ((), ())), preferred_element_type=f32
    )


def contract_first(left, right):
    return lax.dot_general(
        left, right, (((0,), (0,)), ((), ())), preferred_element_type=f32
    )


def lane_of(shape):
    return lax.broadcasted_iota(jnp.int32, shape, len(shape) - 1)


def put_lanes(rows, columns, first=0):
    lane = lane_of((rows, LANES))
    block = jnp.zeros((rows, LANES), f32)
    for place, column in enumerate(columns):
        block = jnp.where(lane == first + place, column, block)
    return block


def halves(value):
    high = value.astype(bf16).astype(f32)
    return high, (value - high).astype(bf16).astype(f32)


def read_lanes(block, first, last):
    lane = lane_of(block.shape)
    inside = (lane >= first) & (lane <= last)
    return jnp.sum(jnp.where(inside, block, 0.0), -1, keepdims=True)


def sum_chunks(parts, start, stop):
    total = parts[0, :, start:stop].astype(f32)
    for chunk in range(1, parts.shape[0]):
        total += parts[chunk, :, start:stop].astype(f32)
    return total


def flat(ref, start, stop):
    return ref[:, :, start:stop].reshape(-1, stop - start)


def own_half(core):
    return pl.ds(pl.multiple_of(core * 512, 512), 512)


def call(kernel, name, outs, *operands, grid_spec=None):
    options = {}
    if grid_spec is None:
        options["in_specs"] = [
            SMEM if space == "s" else VMEM for space, _ in operands
        ]
        options["out_specs"] = [VMEM] * len(outs)
    else:
        options["grid_spec"] = grid_spec
    result = pl.pallas_call(
        kernel,
        out_shape=[jax.ShapeDtypeStruct(shape, dtype) for shape, dtype in outs],
        compiler_params=pltpu.CompilerParams(vmem_limit_bytes=40 * 2**20),
        name=name,
        **options,
    )(*[operand for _, operand in operands])
    return result[0] if len(outs) == 1 else result


def half_out_kernel(core, taps, out):
    sets, _, width = taps.shape
    chunks = width // 1024
    other = (1 - core[0]) * 512
    for s in range(sets):
        for chunk in range(chunks):
            start = pl.multiple_of(chunk * 1024 + other, 512)
            out[s, :, chunk * 512 : (chunk + 1) * 512] = taps[s, :, pl.ds(start, 512)]


def half_join_kernel(core, taps, received, out):
    sets, _, width = taps.shape
    chunks = width // 1024
    copies = out.shape[0] // chunks
    own = core[0] * 512
    first = core[0] == 0
    for chunk in range(chunks):
        rows = []
        for s in range(sets):
            start = pl.multiple_of(chunk * 1024 + own, 512)
            mine = taps[s, :, pl.ds(start, 512)].astype(f32)
            theirs = received[s, :, chunk * 512 : (chunk + 1) * 512].astype(f32)
            rows.append(jnp.where(first, mine, theirs))
            rows.append(jnp.where(first, theirs, mine))
        block = jnp.concatenate(rows, axis=0).astype(bf16)
        for copy in range(copies):
            out[chunk * copies + copy] = block


def join_own_kernel(core, taps, weight, out):
    out[0] = dot(taps[0], weight[0]) + dot(taps[1], weight[1])
    out[1] = dot(taps[2], weight[2])


def join_other_kernel(core, taps, weight, begun, out):
    constant = begun[0] + dot(taps[0], weight[0]) + dot(taps[1], weight[1])
    out[:, :, :512] = constant.astype(bf16).reshape(8, 64, 512)
    top = begun[1] + dot(taps[2], weight[2])
    out[:, :, 512:] = top.astype(bf16).reshape(8, 64, 512)


def join_half(kernel, name, out, core, taps, weight, begun, other):
    whole = lambda i, core: (0, 0, 0)
    half = lambda i, core: (0, (1 - core[0]) if other else core[0], 0)
    specs = [pl.BlockSpec((3, 512, 512), whole), pl.BlockSpec((3, 512, 512), half)]
    operands = [taps, weight]
    if other:
        specs.append(pl.BlockSpec((2, 512, 512), whole))
        operands.append(begun)
    shape, dtype = out
    return pl.pallas_call(
        kernel,
        grid_spec=pltpu.PrefetchScalarGridSpec(
            num_scalar_prefetch=1,
            grid=(1,),
            in_specs=specs,
            out_specs=pl.BlockSpec(shape, whole),
        ),
        out_shape=jax.ShapeDtypeStruct(shape, dtype),
        compiler_params=pltpu.CompilerParams(vmem_limit_bytes=40 * 2**20),
        cost_estimate=pl.CostEstimate(
            flops=2 * 3 * 512**3, bytes_accessed=5 * 2**20, transcendentals=0
        ),
        name=name,
    )(core, *operands)


def write_row_payload(core, joining, gain, payload):
    squares = jnp.sum(joining * joining, -1, keepdims=True)
    payload[:, :512] = (joining * gain[...]).astype(bf16)
    payload[:, 512:] = put_lanes(64, halves(squares), 2 * core[0]).astype(bf16)


def first_rows_kernel(core, got, gain, constant, joining, payload):
    fixed = sum_chunks(got, 0, 512)
    total = fixed + sum_chunks(got, 512, 1024)
    constant[...] = fixed
    joining[...] = total
    write_row_payload(core, total, gain, payload)


def second_rows_kernel(
    core, got, constant, gain, joining, fed_back, logits_first, table, payload
):
    side = sum_chunks(got, 1536, 1664)
    inverse = lax.rsqrt(read_lanes(side, 0, 3) / D + norm_eps)
    fed = inverse * sum_chunks(got, 0, 512)
    total = constant[...] + fed
    fed_back[...] = fed
    joining[...] = total
    write_row_payload(core, total, gain, payload)
    logits_first[...] = inverse * sum_chunks(got, 512, 1536)
    table[...] = put_lanes(64, [inverse, side[:, 4:5], side[:, 5:6]])


def both_halves(core, mine, theirs, weight):
    return dot(flat(mine, 0, 512), weight[own_half(core[0])]) + dot(
        flat(theirs, 0, 512), weight[own_half(1 - core[0])]
    )


def join_second_kernel(core, live, mine, theirs, weight, head, out):
    joined = both_halves(core, mine, theirs, weight.at[0])
    out[:, :, :512] = joined.astype(bf16).reshape(8, 64, 512)
    logits = both_halves(core, mine, theirs, head)
    out[:, :, 512:1536] = logits.astype(bf16).reshape(8, 64, 1024)
    lane = lane_of((8, 64, LANES))
    side = mine[:, :, 512:].astype(f32) + theirs[:, :, 512:].astype(f32)
    side = jnp.where(lane == 4, live[0], jnp.where(lane == 5, live[1], side))
    out[:, :, 1536:] = side.astype(bf16)


def logits_kernel(core, mine, theirs, head, out):
    logits = both_halves(core, mine, theirs, head)
    out[:, :, :1024] = logits.astype(bf16).reshape(8, 64, 1024)
    side = mine[:, :, 512:].astype(f32) + theirs[:, :, 512:].astype(f32)
    out[:, :, 1024:] = side.astype(bf16)


def stats_kernel(base, got, logits_first, targets, logits_second, table, out):
    side = sum_chunks(got, 1024, 1152)
    inverse = lax.rsqrt(read_lanes(side, 0, 3) / D + norm_eps)
    second = inverse * sum_chunks(got, 0, 1024)
    logits_second[...] = second
    table[...] = put_lanes(64, [inverse])
    vocab = lane_of((64, 1024)) + base[0]
    columns = []
    for step, logits in enumerate((logits_first[...], second)):
        top = jnp.max(logits, -1, keepdims=True)
        weights = jnp.exp(logits - top)
        columns += [
            top,
            jnp.sum(weights, -1, keepdims=True),
            jnp.sum(weights * logits, -1, keepdims=True),
            jnp.sum(jnp.where(vocab == targets[step], logits, 0.0), -1, keepdims=True),
        ]
    square = jnp.concatenate([put_lanes(64, columns), jnp.zeros((64, LANES), f32)], 0)
    rows = square.T[:8]
    for copy in range(out.shape[0]):
        out[copy] = rows


def logit_grad_kernel(
    base, shared, logits_first, logits_second, table, targets, masks,
    grads_first, grads_second, turns,
):
    rows = []
    for step in range(STEPS):
        tops = shared[:, 4 * step, :]
        top = jnp.max(tops, 0, keepdims=True)
        factor = jnp.exp(tops - top)
        total = jnp.sum(shared[:, 4 * step + 1, :] * factor, 0, keepdims=True)
        total = jnp.where(total > 0.0, total, 1.0)
        mean = jnp.sum(shared[:, 4 * step + 2, :] * factor, 0, keepdims=True) / total
        picked = jnp.sum(shared[:, 4 * step + 3, :], 0, keepdims=True)
        log_total = top + jnp.log(total)
        rows += [log_total, log_total - picked, mean - picked]
    square = jnp.concatenate(rows + [jnp.zeros((LANES - len(rows), LANES), f32)], 0)
    columns = square.T[:64]
    vocab = lane_of((64, 1024)) + base[0]
    found, loss = [], jnp.zeros((1, 1), f32)
    for step, logits in enumerate((logits_first, logits_second)):
        log_total, entropy, turn = [
            columns[:, 3 * step + i : 3 * step + i + 1] for i in range(3)
        ]
        token_weight = masks[step] / table[:, 1 + step : 2 + step]
        loss += jnp.sum(token_weight * entropy, 0, keepdims=True)
        found.append(token_weight * turn)
        probs = jnp.exp(logits[...] - log_total)
        hit = jnp.where(vocab == targets[step], 1.0, 0.0)
        grad = (token_weight * (probs - hit)).astype(bf16)
        if step == 0:
            grads_first[...] = grad
        else:
            for copy in range(grads_second.shape[0]):
                grads_second[copy] = grad
    turns[...] = put_lanes(64, found + [jnp.broadcast_to(loss, (64, 1))])


def back_second_kernel(
    row_grad, gain, joining, fed_back, table_first, table_second, turns, grads_first, out
):
    inverse = table_second[:, 0:1]
    grad = (
        (inverse * gain[...]) * row_grad[...].astype(f32)
        - (inverse * inverse * turns[:, 1:2] / D) * joining[...]
    ).astype(bf16)
    inner = jnp.sum(grad.astype(f32) * fed_back[...], -1, keepdims=True)
    side = put_lanes(
        64, [*halves(inner), *halves(table_first[:, 0:1]), *halves(turns[:, 2:3])]
    ).astype(bf16)
    logit_grad = grads_first[...]
    for copy in range(out.shape[0]):
        out[copy, :, :512] = grad
        out[copy, :, 512:1536] = logit_grad
        out[copy, :, 1536:] = side


def inner_lanes(core, got):
    side = flat(got, 1536, 1664).astype(f32)
    return put_lanes(512, [side[:, 0:1], side[:, 1:2]], 2 * core[0])


def feed_away_kernel(core, got, weight, head, out):
    rows = own_half(1 - core[0])
    value = contract_last(flat(got, 0, 512), weight[0, rows]) + contract_last(
        flat(got, 512, 1536), head[rows]
    )
    out[:, :, :512] = value.astype(bf16).reshape(8, 64, 512)
    out[:, :, 512:] = inner_lanes(core, got).astype(bf16).reshape(8, 64, LANES)


def feed_keep_kernel(core, got, weight, head, away, out):
    rows = own_half(core[0])
    value = (
        contract_last(flat(got, 0, 512), weight[0, rows])
        + contract_last(flat(got, 512, 1536), head[rows])
        + flat(away, 0, 512).astype(f32)
    )
    out[:, :, :512] = value.astype(bf16).reshape(8, 64, 512)
    side = inner_lanes(core, got) + flat(away, 512, 640).astype(f32)
    out[:, :, 512:] = side.astype(bf16).reshape(8, 64, LANES)


def feed_sum_kernel(landed, out):
    out[:, :512] = sum_chunks(landed, 0, 512).astype(bf16)
    inner = read_lanes(sum_chunks(landed, 512, 640), 0, 3)
    out[:, 512:] = put_lanes(64, halves(inner)).astype(bf16)


def back_first_kernel(row_grad, gain, joining, table, turns, out):
    inverse = table[:, 0:1]
    inner = turns[:, 0:1] + read_lanes(row_grad[:, 512:].astype(f32), 0, 1)
    grad = (
        (inverse * gain[...]) * row_grad[:, :512].astype(f32)
        - (inverse * inverse * inner / D) * joining[...]
    ).astype(bf16)
    for copy in range(out.shape[0]):
        out[copy] = grad


def grad_kernel(
    core, own, other, mine, theirs, first, second, side, grad, squares, folded
):
    tap = pl.program_id(0)
    later = flat(second, 0, 512)

    def both(lefts, rights):
        for half, columns in enumerate(lefts):
            value = sum(contract_first(x, y) for x, y in zip(columns, rights))
            place = core[0] if half == 0 else 1 - core[0]
            grad[0, own_half(place)] = value
            total = jnp.sum((value * value).reshape(-1, 8, 512), 0)
            total = total[:, :128] + total[:, 128:256] + total[:, 256:384] + total[:, 384:]
            folded[...] = total if half == 0 else folded[...] + total

    @pl.when(tap < 2)
    def _():
        both([(own[0], own[0]), (other[0], other[0])], (flat(first, 0, 512), later))

    @pl.when(tap == 2)
    def _():
        inverse = read_lanes(flat(side, 0, LANES).astype(f32), 2, 3)
        scaled = (later.astype(f32) * inverse).astype(bf16)
        both(
            [(own[0], flat(mine, 0, 512)), (other[0], flat(theirs, 0, 512))],
            (flat(first, 0, 512), scaled),
        )

    @pl.when(tap == 0)
    def _():
        squares[...] = folded[...]

    @pl.when(tap > 0)
    def _():
        squares[...] += folded[...]


def gradients(core, own, other, mine, theirs, first, got):
    tap = lambda s, core: (s, 0, 0)
    whole = lambda s, core: (0, 0, 0)
    return pl.pallas_call(
        grad_kernel,
        grid_spec=pltpu.PrefetchScalarGridSpec(
            num_scalar_prefetch=1,
            grid=(3,),
            in_specs=[
                pl.BlockSpec((1, 512, 512), tap),
                pl.BlockSpec((1, 512, 512), tap),
                pl.BlockSpec((8, 64, 512), whole),
                pl.BlockSpec((8, 64, 512), whole),
                pl.BlockSpec((8, 64, 512), whole),
                pl.BlockSpec((8, 64, 512), whole),
                pl.BlockSpec((8, 64, LANES), lambda s, core: (0, 0, 1536 // LANES)),
            ],
            out_specs=[
                pl.BlockSpec((1, 1024, 512), tap),
                pl.BlockSpec((8, LANES), lambda s, core: (0, 0)),
            ],
            scratch_shapes=[pltpu.VMEM((8, LANES), f32)],
        ),
        out_shape=[
            jax.ShapeDtypeStruct((3, 1024, 512), f32),
            jax.ShapeDtypeStruct((8, LANES), f32),
        ],
        compiler_params=pltpu.CompilerParams(vmem_limit_bytes=40 * 2**20),
        cost_estimate=pl.CostEstimate(
            flops=6 * 4 * 512 * 512 * 512, bytes_accessed=10 * 2**20, transcendentals=0
        ),
        name="gradients",
    )(core, own, other, mine, theirs, first, got, got)


def adam_kernel(
    clip, weight, grad, first, second, first_scale, second_scale,
    new_weight, new_first, new_second, new_first_scale, new_second_scale,
):
    rows = weight.shape[1]
    clip_value = clip[0]
    old_scales = jnp.concatenate(
        [first_scale[0], second_scale[0], jnp.zeros((4, rows), f32)], axis=0
    ).T
    new_columns = []
    for block in range(2):
        span = slice(block * BLOCK, (block + 1) * BLOCK)
        clipped = grad[0, :, span] * clip_value
        first_new = (
            first[0, :, span].astype(f32) * (beta_first * old_scales[:, block : block + 1])
            + (1.0 - beta_first) * clipped
        )
        second_new = (
            second[0, :, span].astype(f32)
            * (beta_second * old_scales[:, 2 + block : 3 + block])
            + (1.0 - beta_second) * clipped * clipped
        )
        current = weight[0, :, span].astype(f32)
        spread_sq = second_new * (1.0 / (1.0 - beta_second**step_count))
        spread = spread_sq * lax.rsqrt(spread_sq) + adam_eps
        turned = pl.reciprocal(spread, approx=True)
        turned = turned * (2.0 - spread * turned)
        step = first_new * turned * (learn_rate / (1.0 - beta_first**step_count))
        new_weight[0, :, span] = (
            current * (1.0 - learn_rate * weight_decay) - step
        ).astype(bf16)
        first_top = jnp.max(jnp.abs(first_new), -1, keepdims=True) + scale_eps
        second_top = jnp.max(jnp.abs(second_new), -1, keepdims=True) + scale_eps
        new_first[0, :, span] = (first_new * (1.0 / first_top)).astype(bf16)
        new_second[0, :, span] = (second_new * (1.0 / second_top)).astype(bf16)
        new_columns.append((first_top, second_top))
    lane = lax.broadcasted_iota(jnp.int32, (rows, LANES), 1)
    table = jnp.zeros((rows, LANES), f32)
    for block, (first_top, second_top) in enumerate(new_columns):
        table = jnp.where(lane == block, first_top, table)
        table = jnp.where(lane == 2 + block, second_top, table)
    turned = table.T
    new_first_scale[0] = turned[0:2]
    new_second_scale[0] = turned[2:4]


def adam(clip, weight, grad, first, second, first_scale, second_scale):
    rows = 256
    wide = pl.BlockSpec((1, rows, 512), lambda s, i: (s, i, 0))
    thin = pl.BlockSpec((1, 2, rows), lambda s, i: (s, 0, i))
    return pl.pallas_call(
        adam_kernel,
        grid=(3, 1024 // rows),
        in_specs=[SMEM, wide, wide, wide, wide, thin, thin],
        out_specs=[wide, wide, wide, thin, thin],
        out_shape=[
            jax.ShapeDtypeStruct((3, 1024, 512), bf16),
            jax.ShapeDtypeStruct((3, 1024, 512), bf16),
            jax.ShapeDtypeStruct((3, 1024, 512), bf16),
            jax.ShapeDtypeStruct((3, 2, 1024), f32),
            jax.ShapeDtypeStruct((3, 2, 1024), f32),
        ],
        compiler_params=pltpu.CompilerParams(vmem_limit_bytes=60 * 2**20),
        name="update",
    )(clip, weight, grad, first, second, first_scale, second_scale)


def shards(
    taps, gain, join_weight, head_weight, targets, masks,
    first_codes, first_scales, second_codes, second_scales,
):
    row_count = lax.axis_size("p")
    column_count = lax.axis_size("m")
    core_count = lax.axis_size("b")
    core = lax.axis_index("b")
    core_array = core.reshape(1).astype(jnp.int32)
    turn_pairs = [
        ((p * core_count + b) * column_count + m, (m * core_count + b) * column_count + p)
        for p in range(row_count)
        for b in range(core_count)
        for m in range(column_count)
    ]

    def turn(value):
        return lax.ppermute(value, AXES, turn_pairs)

    def swap(value):
        return lax.ppermute(value, "b", [(0, 1), (1, 0)])

    def exchange(value, axis):
        return lax.all_to_all(value, axis, 0, 0, tiled=False)

    def spread(value, axis):
        copies = lax.axis_size(axis)
        return exchange(jnp.broadcast_to(value, (copies,) + value.shape), axis)

    def own_rows(weight):
        return lax.dynamic_slice_in_dim(weight, core * 512, 512, weight.ndim - 2)

    def other_rows(weight):
        return lax.dynamic_slice_in_dim(weight, (1 - core) * 512, 512, weight.ndim - 2)

    base = (lax.axis_index("p") * core_count + core).reshape(1).astype(jnp.int32) * 1024
    target_ids = targets.reshape(STEPS, 64, 1)
    mask_float = masks.astype(f32).reshape(STEPS, 64, 1)
    live = jnp.sum(masks.astype(f32), axis=(1, 2))
    gain_row = gain.reshape(1, 512)
    row_f32, row_payload = ((64, 512), f32), ((64, 640), bf16)
    table_shape = ((64, LANES), f32)
    last_join = pl.BlockSpec((1, 1024, 512), lambda i: (2, 0, 0))
    scalar = pl.BlockSpec(memory_space=pltpu.SMEM)

    def whole(*shape):
        return pl.BlockSpec(shape, lambda i: (0,) * len(shape))

    def one_step(specs, out):
        return pl.GridSpec(grid=(1,), in_specs=specs, out_specs=[out])

    with jax.named_scope("taps_in"):
        outgoing = call(
            half_out_kernel, "half_out", [((3, 4, D // 2), bf16)],
            ("s", core_array), ("v", taps),
        )
        incoming = swap(outgoing)
        packed = call(
            half_join_kernel, "half_join", [((64, 24, 512), bf16)],
            ("s", core_array), ("v", taps), ("v", incoming),
        )
        landed = exchange(packed, ("m", "p"))
        taps_own = landed.reshape(64, 3, 8, 512).transpose(1, 0, 2, 3).reshape(3, 512, 512)
        taps_other = swap(taps_own)

    with jax.named_scope("join_first"):
        begun = join_half(
            join_own_kernel, "join_own", ((2, 512, 512), f32),
            core_array, taps_own, join_weight, None, False,
        )
        parts = join_half(
            join_other_kernel, "join_other", ((8, 64, 1024), bf16),
            core_array, taps_other, join_weight, begun, True,
        )
        constant, joining_first, payload = call(
            first_rows_kernel, "first_rows", [row_f32, row_f32, row_payload],
            ("s", core_array), ("v", exchange(parts, "m")), ("v", gain_row),
        )

    with jax.named_scope("hidden_first"):
        hidden_mine = spread(turn(payload), "p")
        hidden_theirs = swap(hidden_mine)

    with jax.named_scope("join_second"):
        parts = call(
            join_second_kernel, "join_second", [((8, 64, 1664), bf16)],
            ("s", core_array), ("s", live), ("v", hidden_mine), ("v", hidden_theirs),
            ("v", join_weight), ("v", head_weight),
            grid_spec=one_step(
                [
                    scalar, scalar, whole(8, 64, 640), whole(8, 64, 640),
                    last_join, whole(1024, 1024),
                ],
                whole(8, 64, 1664),
            ),
        )
        joining_second, fed_back, logits_first, table_first, payload = call(
            second_rows_kernel, "second_rows",
            [row_f32, row_f32, ((64, 1024), f32), table_shape, row_payload],
            ("s", core_array), ("v", exchange(parts, "m")), ("v", constant),
            ("v", gain_row),
        )

    with jax.named_scope("hidden_second"):
        later_mine = spread(turn(payload), "p")
        later_theirs = swap(later_mine)

    with jax.named_scope("logits"):
        parts = call(
            logits_kernel, "logits", [((8, 64, 1152), bf16)],
            ("s", core_array), ("v", later_mine), ("v", later_theirs), ("v", head_weight),
        )
        got = exchange(parts, "m")

    with jax.named_scope("softmax"):
        logits_second, table_second, stats = call(
            stats_kernel, "stats",
            [((64, 1024), f32), table_shape, ((row_count * core_count, 8, LANES), f32)],
            ("s", base), ("v", got), ("v", logits_first), ("v", target_ids),
        )
        shared = exchange(stats, ("p", "b"))
        grads_first, grad_copies, turns = call(
            logit_grad_kernel, "logit_grad",
            [((64, 1024), bf16), ((column_count, 64, 1024), bf16), table_shape],
            ("s", base), ("v", shared), ("v", logits_first), ("v", logits_second),
            ("v", table_first), ("v", target_ids), ("v", mask_float),
        )
        grads_second = exchange(grad_copies, "m").reshape(512, 1024)

    with jax.named_scope("back_second"):
        away = swap(contract_last(grads_second, other_rows(head_weight)).astype(bf16))
        kept = contract_last(grads_second, own_rows(head_weight)) + away.astype(f32)
        landed = exchange(kept.astype(bf16).reshape(8, 64, 512), "p")
        row_grad = turn(jnp.sum(landed.astype(f32), 0).astype(bf16))
        payload = call(
            back_second_kernel, "back_second", [((column_count, 64, 1664), bf16)],
            ("v", row_grad), ("v", gain_row), ("v", joining_second), ("v", fed_back),
            ("v", table_first), ("v", table_second), ("v", turns), ("v", grads_first),
        )
        got = exchange(payload, "m")

    with jax.named_scope("back_first"):
        weights = (("v", join_weight), ("v", head_weight))
        specs = [scalar, whole(8, 64, 1664), last_join, whole(1024, 1024)]
        away = swap(
            call(
                feed_away_kernel, "feed_away", [((8, 64, 640), bf16)],
                ("s", core_array), ("v", got), *weights,
                grid_spec=one_step(specs, whole(8, 64, 640)),
            )
        )
        parts = call(
            feed_keep_kernel, "feed_keep", [((8, 64, 640), bf16)],
            ("s", core_array), ("v", got), *weights, ("v", away),
            grid_spec=one_step(specs + [whole(8, 64, 640)], whole(8, 64, 640)),
        )
        summed = call(
            feed_sum_kernel, "feed_sum", [row_payload], ("v", exchange(parts, "p"))
        )
        copies = call(
            back_first_kernel, "back_first", [((column_count, 64, 512), bf16)],
            ("v", turn(summed)), ("v", gain_row), ("v", joining_first),
            ("v", table_first), ("v", turns),
        )
        first_all = exchange(copies, "m")

    with jax.named_scope("gradients"):
        grads, squares = gradients(
            core_array, taps_own, taps_other, hidden_mine, hidden_theirs, first_all, got
        )
        square_sum = jnp.broadcast_to(jnp.sum(squares), (1, LANES))
        norm_sq = jnp.sum(spread(square_sum, AXES)[:, 0, 0])
        clip = jnp.minimum(1.0, clip_norm / (jnp.sqrt(norm_sq) + 1e-06))

    with jax.named_scope("update"):
        new_join, new_first, new_second, first_scale, second_scale = adam(
            clip.reshape(1),
            join_weight,
            grads,
            first_codes,
            second_codes,
            jnp.swapaxes(first_scales, 1, 2),
            jnp.swapaxes(second_scales, 1, 2),
        )
        loss = jnp.sum(got[:, 0, 1540:1542].astype(f32))
    return (
        new_join,
        new_first,
        jnp.swapaxes(first_scale, 1, 2),
        new_second,
        jnp.swapaxes(second_scale, 1, 2),
        loss,
    )


def solution(mesh):
    rows = mesh.shape["dp"] // 2
    fine = Mesh(mesh.devices.reshape(rows, 2, mesh.shape["mp"]), AXES)
    dp, mp = ("p", "b"), "m"
    return jax.shard_map(
        shards,
        mesh=fine,
        in_specs=(
            P(None, ("p", "b", "m"), None),
            P(dp),
            P(None, mp, dp),
            P(mp, dp),
            P(None, None, mp),
            P(None, None, mp),
            P(None, mp, dp),
            P(None, mp, dp),
            P(None, mp, dp),
            P(None, mp, dp),
        ),
        out_specs=(
            P(None, mp, dp),
            P(None, mp, dp),
            P(None, mp, dp),
            P(None, mp, dp),
            P(None, mp, dp),
            P(),
        ),
        check_vma=False,
    )
```

```python
import jax
import jax.numpy as jnp
from jax import lax
from jax.experimental import pallas as pl
from jax.experimental.pallas import tpu as pltpu
from jax.sharding import Mesh, PartitionSpec as P

D = 8192
STEPS = 2
BLOCK = 256
LANES = 128
CHUNKS = 8

norm_eps = 1e-05
clip_norm = 1.0
learn_rate = 0.0003
weight_decay = 0.1
beta_first = 0.9
beta_second = 0.999
step_count = 10.0
adam_eps = 1e-08
scale_eps = 1e-12

bf16 = jnp.bfloat16
f32 = jnp.float32
AXES = ("p", "b", "m")
VMEM = pl.BlockSpec(memory_space=pltpu.VMEM)
SMEM = pl.BlockSpec(memory_space=pltpu.SMEM)


def dot(left, right):
    return jnp.dot(left, right, preferred_element_type=f32)


def contract_last(left, right):
    return lax.dot_general(
        left, right, (((1,), (1,)), ((), ())), preferred_element_type=f32
    )


def contract_first(left, right):
    return lax.dot_general(
        left, right, (((0,), (0,)), ((), ())), preferred_element_type=f32
    )


def put_lanes(rows, columns):
    lane = lax.broadcasted_iota(jnp.int32, (rows, LANES), 1)
    block = jnp.zeros((rows, LANES), f32)
    for place, column in enumerate(columns):
        block = jnp.where(lane == place, column, block)
    return block


def total_over(parts, picks, start, stop):
    total = parts[picks[0], :, start:stop].astype(f32)
    for pick in picks[1:]:
        total += parts[pick, :, start:stop].astype(f32)
    return total


def column_sum(parts, row, start, stop):
    return total_over(parts, [row * CHUNKS + m for m in range(CHUNKS)], start, stop)


def row_sum(parts, column, start, stop):
    return total_over(parts, [p * CHUNKS + column for p in range(CHUNKS)], start, stop)


def lane_total(values):
    total = values[0]
    for value in values[1:]:
        total = total + value
    return jnp.broadcast_to(jnp.sum(total, -1, keepdims=True), (8, LANES))


def to_blocks(value):
    return value.reshape(64, 8, value.shape[-1]).astype(bf16)


def half_rows(core):
    return pl.ds(pl.multiple_of(core * 512, 512), 512)


def call(kernel, name, outs, *operands, specs=None, flops=0):
    options = {}
    if specs is None:
        options["in_specs"] = [SMEM if space == "s" else VMEM for space, _ in operands]
        options["out_specs"] = [VMEM] * len(outs)
    else:
        options["grid_spec"] = pltpu.PrefetchScalarGridSpec(
            num_scalar_prefetch=1,
            grid=(1,),
            in_specs=specs,
            out_specs=[whole_block(shape) for shape, _ in outs],
        )
    result = pl.pallas_call(
        kernel,
        out_shape=[jax.ShapeDtypeStruct(shape, dtype) for shape, dtype in outs],
        compiler_params=pltpu.CompilerParams(vmem_limit_bytes=40 * 2**20),
        cost_estimate=pl.CostEstimate(
            flops=flops, bytes_accessed=4 * 2**20, transcendentals=0
        ),
        name=name,
        **options,
    )(*[operand for _, operand in operands])
    return result[0] if len(outs) == 1 else result


def whole_block(shape):
    return pl.BlockSpec(shape, lambda i, core: (0,) * len(shape))


def half_out_kernel(core, taps, out):
    sets, _, width = taps.shape
    chunks = width // 1024
    other = (1 - core[0]) * 512
    for s in range(sets):
        for chunk in range(chunks):
            start = pl.multiple_of(chunk * 1024 + other, 512)
            out[s, :, chunk * 512 : (chunk + 1) * 512] = taps[s, :, pl.ds(start, 512)]


def half_join_kernel(core, taps, received, out):
    sets, _, width = taps.shape
    chunks = width // 1024
    copies = out.shape[0] // chunks
    own = core[0] * 512
    first = core[0] == 0
    for chunk in range(chunks):
        rows = []
        for s in range(sets):
            start = pl.multiple_of(chunk * 1024 + own, 512)
            mine = taps[s, :, pl.ds(start, 512)].astype(f32)
            theirs = received[s, :, chunk * 512 : (chunk + 1) * 512].astype(f32)
            rows.append(jnp.where(first, mine, theirs))
            rows.append(jnp.where(first, theirs, mine))
        block = jnp.concatenate(rows, axis=0).astype(bf16)
        for copy in range(copies):
            out[copy * chunks + chunk] = block


def join_own_kernel(core, taps, weight, out):
    out[0] = dot(taps[0], weight[0]) + dot(taps[1], weight[1])
    out[1] = dot(taps[2], weight[2])


def join_other_kernel(core, taps, weight, begun, side, constant, out):
    fixed = begun[0] + dot(taps[0], weight[0]) + dot(taps[1], weight[1])
    constant[...] = fixed
    out[:, :, :512] = to_blocks(fixed + begun[1] + dot(taps[2], weight[2]))
    out[:, :, 512:] = jnp.broadcast_to(side[...], (64, 8, LANES)).astype(bf16)


def both_halves(core, mine, theirs, weight):
    return dot(mine[...], weight[half_rows(core[0])]) + dot(
        theirs[...], weight[half_rows(1 - core[0])]
    )


def join_second_kernel(core, mine, theirs, weight, head, constant, out):
    joined = constant[...] + both_halves(core, mine, theirs, weight.at[0])
    out[:, :, :512] = to_blocks(joined)
    out[:, :, 512:] = to_blocks(both_halves(core, mine, theirs, head))


def logits_kernel(core, mine, theirs, head, out):
    out[...] = to_blocks(both_halves(core, mine, theirs, head))


def head_back_kernel(core, grads, head, *rest):
    *added, out = rest
    value = contract_last(grads[...], head[half_rows(core[0])])
    if added:
        value += added[0][...].astype(f32).reshape(512, 512)
    out[...] = to_blocks(value)


def feed_back_kernel(core, got, weight, head, *rest):
    *added, out = rest
    rows = half_rows(core[0])
    value = contract_last(got[:, :512], weight[0, rows])
    value += contract_last(got[:, 512:], head[rows])
    if added:
        value += added[0][...].astype(f32).reshape(512, 512)
    out[...] = to_blocks(value)


def first_rows_kernel(got, joining, gain, counts, squares):
    terms = []
    for chunk in range(CHUNKS):
        value = column_sum(got, chunk, 0, 512)
        joining[chunk] = value
        terms.append(value * value)
        side = total_over(got, [chunk * CHUNKS, chunk * CHUNKS + 1], 512, 640)
        row = jnp.concatenate([side[i : i + 1] for i in range(4)], axis=1)
        gain[chunk] = jnp.broadcast_to(row, (8, 512))
    squares[...] = lane_total(terms)
    counts[...] = jnp.broadcast_to(column_sum(got, 0, 512, 640)[4:5], (8, LANES))


def second_rows_kernel(got, joining, logits, squares):
    terms = []
    for chunk in range(CHUNKS):
        value = column_sum(got, chunk, 0, 512)
        joining[chunk] = value
        terms.append(value * value)
        logits[chunk] = column_sum(got, chunk, 512, 1536)
    squares[...] = lane_total(terms)


def norm_kernel(joining, gain, squares, squares_other, inverse, out):
    factor = lax.rsqrt((squares[...] + squares_other[...]) / D + norm_eps)
    inverse[...] = factor
    for chunk in range(CHUNKS):
        hidden = (joining[chunk] * factor[:, 0:1] * gain[chunk]).astype(bf16)
        for copy in range(CHUNKS):
            out[copy * CHUNKS + chunk] = hidden


def norm_inner_kernel(got, joining, gain, scaled, inner):
    terms = []
    for chunk in range(CHUNKS):
        value = row_sum(got, chunk, 0, 512) * gain[chunk]
        scaled[chunk] = value
        terms.append(value * joining[chunk])
    inner[...] = lane_total(terms)


def norm_back_kernel(scaled, joining, inverse, inner, inner_other, *rest):
    *riders, out = rest
    factor = inverse[:, 0:1]
    pull = factor * factor * factor * (inner[:, 0:1] + inner_other[:, 0:1]) / D
    for chunk in range(CHUNKS):
        grad = (factor * scaled[chunk] - pull * joining[chunk]).astype(bf16)
        for copy in range(CHUNKS):
            out[chunk * CHUNKS + copy, :, :512] = grad
            if riders:
                out[chunk * CHUNKS + copy, :, 512:] = riders[0][chunk]


def vocab_of(core, chunk):
    return lax.broadcasted_iota(jnp.int32, (8, 1024), 1) + (2 * chunk + core) * 1024


def stats_kernel(core, got, logits_first, targets, logits_second, stats):
    for chunk in range(CHUNKS):
        logits_second[chunk] = column_sum(got, chunk, 0, 1024)
    columns = []
    for step, logits in enumerate((logits_first, logits_second)):
        top = logits[0]
        for chunk in range(1, CHUNKS):
            top = jnp.maximum(top, logits[chunk])
        top = jnp.max(top, -1, keepdims=True)
        weights = jnp.zeros((8, 1024), f32)
        picked = jnp.zeros((8, 1024), f32)
        for chunk in range(CHUNKS):
            weights += jnp.exp(logits[chunk] - top)
            hit = vocab_of(core[0], chunk) == targets[step]
            picked += jnp.where(hit, logits[chunk], 0.0)
        columns += [
            top,
            jnp.sum(weights, -1, keepdims=True),
            jnp.sum(picked, -1, keepdims=True),
        ]
    stats[...] = put_lanes(8, columns)


def logit_grad_kernel(
    core, stats, stats_other, logits_first, logits_second, targets, masks, counts,
    grads_first, grads_second, loss,
):
    lost = jnp.zeros((8, 1), f32)
    for step, logits in enumerate((logits_first, logits_second)):
        place = 3 * step
        top_mine, top_other = [x[:, place : place + 1] for x in (stats, stats_other)]
        sum_mine, sum_other = [
            x[:, place + 1 : place + 2] for x in (stats, stats_other)
        ]
        picked = stats[:, place + 2 : place + 3] + stats_other[:, place + 2 : place + 3]
        top = jnp.maximum(top_mine, top_other)
        total = sum_mine * jnp.exp(top_mine - top) + sum_other * jnp.exp(top_other - top)
        log_total = top + jnp.log(total)
        weight = masks[step] / counts[:, step : step + 1]
        lost += weight * (log_total - picked)
        for chunk in range(CHUNKS):
            probs = jnp.exp(logits[chunk] - log_total)
            hit = jnp.where(vocab_of(core[0], chunk) == targets[step], 1.0, 0.0)
            grad = (weight * (probs - hit)).astype(bf16)
            if step == 0:
                grads_first[chunk] = grad
            else:
                for copy in range(CHUNKS):
                    grads_second[chunk * CHUNKS + copy] = grad
    once = jnp.where(core[0] == 0, 1.0, 0.0)
    loss[...] = jnp.broadcast_to(jnp.sum(lost, 0, keepdims=True) * once, (8, LANES))


def grad_kernel(core, own, other, mine, theirs, first, second, loss, grad, totals):
    tap = pl.program_id(0)

    def both(lefts):
        for half, (left, left_later) in enumerate(lefts):
            value = contract_first(left, first[...]) + contract_first(
                left_later, second[...]
            )
            grad[0, half_rows(core[0] if half == 0 else 1 - core[0])] = value
            total = jnp.sum((value * value).reshape(-1, 8, 512), 0)
            total = total[:, :128] + total[:, 128:256] + total[:, 256:384] + total[:, 384:]
            totals[0] += total

    @pl.when(tap == 0)
    def _():
        totals[0] = jnp.zeros((8, LANES), f32)
        totals[1] = loss[...]

    @pl.when(tap < 2)
    def _():
        both([(own[0], own[0]), (other[0], other[0])])

    @pl.when(tap == 2)
    def _():
        both([(own[0], mine[...]), (other[0], theirs[...])])


def gradients(core, own, other, mine, theirs, first, got, loss):
    tap = lambda s, core: (s, 0, 0)
    still = pl.BlockSpec((512, 512), lambda s, core: (0, 0))
    return pl.pallas_call(
        grad_kernel,
        grid_spec=pltpu.PrefetchScalarGridSpec(
            num_scalar_prefetch=1,
            grid=(3,),
            in_specs=[
                pl.BlockSpec((1, 512, 512), tap),
                pl.BlockSpec((1, 512, 512), tap),
                still,
                still,
                still,
                still,
                pl.BlockSpec((8, LANES), lambda s, core: (0, 0)),
            ],
            out_specs=[
                pl.BlockSpec((1, 1024, 512), tap),
                pl.BlockSpec((2, 8, LANES), lambda s, core: (0, 0, 0)),
            ],
        ),
        out_shape=[
            jax.ShapeDtypeStruct((3, 1024, 512), f32),
            jax.ShapeDtypeStruct((2, 8, LANES), f32),
        ],
        compiler_params=pltpu.CompilerParams(vmem_limit_bytes=40 * 2**20),
        cost_estimate=pl.CostEstimate(
            flops=6 * 4 * 512 * 512 * 512, bytes_accessed=10 * 2**20, transcendentals=0
        ),
        name="gradients",
    )(core, own, other, mine, theirs, first, got, loss)


def adam_kernel(
    clip, weight, grad, first, second, first_scale, second_scale,
    new_weight, new_first, new_second, new_first_scale, new_second_scale,
):
    rows = weight.shape[1]
    clip_value = clip[0]
    old_scales = jnp.concatenate(
        [first_scale[0], second_scale[0], jnp.zeros((4, rows), f32)], axis=0
    ).T
    new_columns = []
    for block in range(2):
        span = slice(block * BLOCK, (block + 1) * BLOCK)
        clipped = grad[0, :, span] * clip_value
        first_new = (
            first[0, :, span].astype(f32) * (beta_first * old_scales[:, block : block + 1])
            + (1.0 - beta_first) * clipped
        )
        second_new = (
            second[0, :, span].astype(f32)
            * (beta_second * old_scales[:, 2 + block : 3 + block])
            + (1.0 - beta_second) * clipped * clipped
        )
        current = weight[0, :, span].astype(f32)
        spread_sq = second_new * (1.0 / (1.0 - beta_second**step_count))
        spread = spread_sq * lax.rsqrt(spread_sq) + adam_eps
        turned = pl.reciprocal(spread, approx=True)
        turned = turned * (2.0 - spread * turned)
        step = first_new * turned * (learn_rate / (1.0 - beta_first**step_count))
        new_weight[0, :, span] = (
            current * (1.0 - learn_rate * weight_decay) - step
        ).astype(bf16)
        first_top = jnp.max(jnp.abs(first_new), -1, keepdims=True) + scale_eps
        second_top = jnp.max(jnp.abs(second_new), -1, keepdims=True) + scale_eps
        new_first[0, :, span] = (first_new * (1.0 / first_top)).astype(bf16)
        new_second[0, :, span] = (second_new * (1.0 / second_top)).astype(bf16)
        new_columns.append((first_top, second_top))
    lane = lax.broadcasted_iota(jnp.int32, (rows, LANES), 1)
    table = jnp.zeros((rows, LANES), f32)
    for block, (first_top, second_top) in enumerate(new_columns):
        table = jnp.where(lane == block, first_top, table)
        table = jnp.where(lane == 2 + block, second_top, table)
    turned = table.T
    new_first_scale[0] = turned[0:2]
    new_second_scale[0] = turned[2:4]


def adam(clip, weight, grad, first, second, first_scale, second_scale):
    rows = 256
    wide = pl.BlockSpec((1, rows, 512), lambda s, i: (s, i, 0))
    thin = pl.BlockSpec((1, 2, rows), lambda s, i: (s, 0, i))
    return pl.pallas_call(
        adam_kernel,
        grid=(3, 1024 // rows),
        in_specs=[SMEM, wide, wide, wide, wide, thin, thin],
        out_specs=[wide, wide, wide, thin, thin],
        out_shape=[
            jax.ShapeDtypeStruct((3, 1024, 512), bf16),
            jax.ShapeDtypeStruct((3, 1024, 512), bf16),
            jax.ShapeDtypeStruct((3, 1024, 512), bf16),
            jax.ShapeDtypeStruct((3, 2, 1024), f32),
            jax.ShapeDtypeStruct((3, 2, 1024), f32),
        ],
        compiler_params=pltpu.CompilerParams(vmem_limit_bytes=60 * 2**20),
        name="update",
    )(clip, weight, grad, first, second, first_scale, second_scale)


def shards(
    taps, gain, join_weight, head_weight, targets, masks,
    first_codes, first_scales, second_codes, second_scales,
):
    core = lax.axis_index("b")
    row = lax.axis_index("p")
    column = lax.axis_index("m")
    own = core.reshape(1).astype(jnp.int32)
    other = 1 - own
    chips = ("p", "m")

    def swap(value):
        return lax.ppermute(value, "b", [(0, 1), (1, 0)])

    def exchange(value, axes=chips):
        return lax.all_to_all(value, axes, 0, 0, tiled=False)

    def own_tokens(values):
        mine = lax.dynamic_slice_in_dim(values, 2 * row, 2, 1)
        return mine.reshape(STEPS, 8, 1)

    target_ids = own_tokens(targets)
    mask_float = own_tokens(masks).astype(f32)
    gain_rows = gain.reshape(4, LANES)
    gain_high = lax.reduce_precision(gain_rows, 8, 7)
    live = jnp.sum(masks.astype(f32), axis=(1, 2)).reshape(1, STEPS)
    side = jnp.concatenate(
        [
            jnp.where(column % 2 == 0, gain_high, gain_rows - gain_high),
            jnp.pad(live, ((0, 3), (0, LANES - STEPS))),
        ]
    )
    rows_f32, table = ((CHUNKS, 8, 512), f32), ((8, LANES), f32)
    vocab_f32 = ((CHUNKS, 8, 1024), f32)
    blocks = ((64, 8, 512), bf16)
    half_flops = 2 * 512**3
    last_join = pl.BlockSpec((1, 1024, 512), lambda i, core: (2, 0, 0))
    tokens_half, tokens_wide = whole_block((512, 512)), whole_block((512, 1024))
    head_block, parts_block = whole_block((1024, 1024)), whole_block((64, 8, 512))

    with jax.named_scope("taps_in"):
        outgoing = call(
            half_out_kernel, "half_out", [((3, 4, D // 2), bf16)], ("s", own), ("v", taps)
        )
        packed = call(
            half_join_kernel, "half_join", [((64, 24, 512), bf16)],
            ("s", own), ("v", taps), ("v", swap(outgoing)),
        )
        landed = exchange(packed)
        taps_own = landed.reshape(64, 3, 8, 512).transpose(1, 0, 2, 3).reshape(3, 512, 512)
        taps_other = swap(taps_own)

    with jax.named_scope("join_first"):
        sets = whole_block((3, 512, 512))
        begun = call(
            join_own_kernel, "join_own", [((2, 512, 512), f32)],
            ("s", own), ("v", taps_own), ("v", join_weight),
            specs=[sets, pl.BlockSpec((3, 512, 512), lambda i, core: (0, core[0], 0))],
            flops=3 * half_flops,
        )
        constant, parts = call(
            join_other_kernel, "join_other",
            [((512, 512), f32), ((64, 8, 640), bf16)],
            ("s", other), ("v", taps_other), ("v", join_weight), ("v", begun), ("v", side),
            specs=[
                sets,
                pl.BlockSpec((3, 512, 512), lambda i, core: (0, core[0], 0)),
                whole_block((2, 512, 512)),
                whole_block((8, LANES)),
            ],
            flops=3 * half_flops,
        )
        joining_first, gains, counts, squares = call(
            first_rows_kernel, "first_rows", [rows_f32, rows_f32, table, table],
            ("v", exchange(parts)),
        )

    def to_hidden(joining, squares):
        inverse, copies = call(
            norm_kernel, "norm", [table, blocks],
            ("v", joining), ("v", gains), ("v", squares), ("v", swap(squares)),
        )
        mine = exchange(copies).reshape(512, 512)
        return inverse, mine, swap(mine)

    with jax.named_scope("hidden_first"):
        inverse_first, hidden_mine, hidden_theirs = to_hidden(joining_first, squares)

    with jax.named_scope("join_second"):
        parts = call(
            join_second_kernel, "join_second", [((64, 8, 1536), bf16)],
            ("s", own), ("v", hidden_mine), ("v", hidden_theirs), ("v", join_weight),
            ("v", head_weight), ("v", constant),
            specs=[tokens_half, tokens_half, last_join, head_block, tokens_half],
            flops=6 * half_flops,
        )
        joining_second, logits_first, squares = call(
            second_rows_kernel, "second_rows", [rows_f32, vocab_f32, table],
            ("v", exchange(parts)),
        )

    with jax.named_scope("hidden_second"):
        inverse_second, later_mine, later_theirs = to_hidden(joining_second, squares)

    with jax.named_scope("logits"):
        parts = call(
            logits_kernel, "logits", [((64, 8, 1024), bf16)],
            ("s", own), ("v", later_mine), ("v", later_theirs), ("v", head_weight),
            specs=[tokens_half, tokens_half, head_block],
            flops=4 * half_flops,
        )
        got = exchange(parts)

    with jax.named_scope("softmax"):
        logits_second, stats = call(
            stats_kernel, "stats", [vocab_f32, table],
            ("s", own), ("v", got), ("v", logits_first), ("v", target_ids),
        )
        grads_first, copies, loss = call(
            logit_grad_kernel, "logit_grad",
            [((CHUNKS, 8, 1024), bf16), ((64, 8, 1024), bf16), table],
            ("s", own), ("v", stats), ("v", swap(stats)), ("v", logits_first),
            ("v", logits_second), ("v", target_ids), ("v", mask_float), ("v", counts),
        )
        grads_second = exchange(copies).reshape(512, 1024)

    def row_gradients(parts, joining, inverse, *riders):
        scaled, inner = call(
            norm_inner_kernel, "norm_inner", [rows_f32, table],
            ("v", exchange(parts)), ("v", joining), ("v", gains),
        )
        width = 512 + sum(rider.shape[-1] for rider in riders)
        copies = call(
            norm_back_kernel, "norm_back", [((64, 8, width), bf16)],
            ("v", scaled), ("v", joining), ("v", inverse), ("v", inner),
            ("v", swap(inner)), *[("v", rider) for rider in riders],
        )
        return exchange(copies).reshape(512, width)

    with jax.named_scope("back_second"):
        specs, operands = [tokens_wide, head_block], (("v", grads_second), ("v", head_weight))
        away = call(
            head_back_kernel, "head_away", [blocks], ("s", other), *operands,
            specs=specs, flops=2 * half_flops,
        )
        parts = call(
            head_back_kernel, "head_keep", [blocks], ("s", own), *operands,
            ("v", swap(away)), specs=specs + [parts_block], flops=2 * half_flops,
        )
        got = row_gradients(parts, joining_second, inverse_second, grads_first)

    with jax.named_scope("back_first"):
        specs = [whole_block((512, 1536)), last_join, head_block]
        operands = (("v", got), ("v", join_weight), ("v", head_weight))
        away = call(
            feed_back_kernel, "feed_away", [blocks], ("s", other), *operands,
            specs=specs, flops=3 * half_flops,
        )
        parts = call(
            feed_back_kernel, "feed_keep", [blocks], ("s", own), *operands,
            ("v", swap(away)), specs=specs + [parts_block], flops=3 * half_flops,
        )
        first_all = row_gradients(parts, joining_first, inverse_first)

    with jax.named_scope("gradients"):
        grads, totals = gradients(
            own, taps_own, taps_other, hidden_mine, hidden_theirs, first_all, got, loss
        )
        square_sum = jnp.broadcast_to(jnp.sum(totals[0]), (1, LANES))
        lane = lax.broadcasted_iota(jnp.int32, (1, LANES), 1)
        shared = jnp.where(lane == 0, square_sum, totals[1, 0:1])
        shared = exchange(jnp.broadcast_to(shared, (128, 1, LANES)), AXES)
        shared = jnp.sum(shared[:, 0, 0:2], 0)
        clip = jnp.minimum(1.0, clip_norm / (jnp.sqrt(shared[0]) + 1e-06))
        loss = shared[1]

    with jax.named_scope("update"):
        new_join, new_first, new_second, first_scale, second_scale = adam(
            clip.reshape(1),
            join_weight,
            grads,
            first_codes,
            second_codes,
            jnp.swapaxes(first_scales, 1, 2),
            jnp.swapaxes(second_scales, 1, 2),
        )
    return (
        new_join,
        new_first,
        jnp.swapaxes(first_scale, 1, 2),
        new_second,
        jnp.swapaxes(second_scale, 1, 2),
        loss,
    )


def solution(mesh):
    rows = mesh.shape["dp"] // 2
    fine = Mesh(mesh.devices.reshape(rows, 2, mesh.shape["mp"]), AXES)
    dp, mp = ("p", "b"), "m"
    return jax.shard_map(
        shards,
        mesh=fine,
        in_specs=(
            P(None, ("p", "b", "m"), None),
            P(dp),
            P(None, mp, dp),
            P(mp, dp),
            P(None, None, mp),
            P(None, None, mp),
            P(None, mp, dp),
            P(None, mp, dp),
            P(None, mp, dp),
            P(None, mp, dp),
        ),
        out_specs=(
            P(None, mp, dp),
            P(None, mp, dp),
            P(None, mp, dp),
            P(None, mp, dp),
            P(None, mp, dp),
            P(),
        ),
        check_vma=False,
    )
```

```python
import jax
import jax.numpy as jnp
from jax import lax
from jax.experimental import pallas as pl
from jax.experimental.pallas import tpu as pltpu
from jax.sharding import Mesh, PartitionSpec as P

D = 8192
STEPS = 2
BLOCK = 256
LANES = 128
CHUNKS = 8

norm_eps = 1e-05
clip_norm = 1.0
learn_rate = 0.0003
weight_decay = 0.1
beta_first = 0.9
beta_second = 0.999
step_count = 10.0
adam_eps = 1e-08
scale_eps = 1e-12

bf16 = jnp.bfloat16
f32 = jnp.float32
AXES = ("p", "b", "m")
VMEM = pl.BlockSpec(memory_space=pltpu.VMEM)
SMEM = pl.BlockSpec(memory_space=pltpu.SMEM)


def dot(left, right):
    return jnp.dot(left, right, preferred_element_type=f32)


def contract_last(left, right):
    return lax.dot_general(
        left, right, (((1,), (1,)), ((), ())), preferred_element_type=f32
    )


def contract_first(left, right):
    return lax.dot_general(
        left, right, (((0,), (0,)), ((), ())), preferred_element_type=f32
    )


def put_lanes(rows, columns):
    lane = lax.broadcasted_iota(jnp.int32, (rows, LANES), 1)
    block = jnp.zeros((rows, LANES), f32)
    for place, column in enumerate(columns):
        block = jnp.where(lane == place, column, block)
    return block


def total_over(parts, picks, start, stop):
    total = parts[picks[0], :, start:stop].astype(f32)
    for pick in picks[1:]:
        total += parts[pick, :, start:stop].astype(f32)
    return total


def column_sum(parts, row, start, stop):
    return total_over(parts, [row * CHUNKS + m for m in range(CHUNKS)], start, stop)


def row_sum(parts, column, start, stop):
    return total_over(parts, [p * CHUNKS + column for p in range(CHUNKS)], start, stop)


def lane_total(values):
    total = values[0]
    for value in values[1:]:
        total = total + value
    return jnp.broadcast_to(jnp.sum(total, -1, keepdims=True), (8, LANES))


def to_blocks(value):
    return value.reshape(64, 8, value.shape[-1]).astype(bf16)


def half_rows(core):
    return pl.ds(pl.multiple_of(core * 512, 512), 512)


def call(kernel, name, outs, *operands, specs=None, flops=0):
    options = {}
    if specs is None:
        options["in_specs"] = [SMEM if space == "s" else VMEM for space, _ in operands]
        options["out_specs"] = [VMEM] * len(outs)
    else:
        options["grid_spec"] = pltpu.PrefetchScalarGridSpec(
            num_scalar_prefetch=1,
            grid=(1,),
            in_specs=specs,
            out_specs=[whole_block(shape) for shape, _ in outs],
        )
    result = pl.pallas_call(
        kernel,
        out_shape=[jax.ShapeDtypeStruct(shape, dtype) for shape, dtype in outs],
        compiler_params=pltpu.CompilerParams(vmem_limit_bytes=24 * 2**20),
        cost_estimate=pl.CostEstimate(
            flops=flops, bytes_accessed=4 * 2**20, transcendentals=0
        ),
        name=name,
        **options,
    )(*[operand for _, operand in operands])
    return result[0] if len(outs) == 1 else result


def whole_block(shape):
    return pl.BlockSpec(shape, lambda i, core: (0,) * len(shape))


def half_out_kernel(core, taps, out):
    sets, _, width = taps.shape
    chunks = width // 1024
    other = (1 - core[0]) * 512
    for s in range(sets):
        for chunk in range(chunks):
            start = pl.multiple_of(chunk * 1024 + other, 512)
            out[s, :, chunk * 512 : (chunk + 1) * 512] = taps[s, :, pl.ds(start, 512)]


def half_join_kernel(core, taps, received, out):
    sets, _, width = taps.shape
    chunks = width // 1024
    copies = out.shape[0] // chunks
    own = core[0] * 512
    first = core[0] == 0
    for chunk in range(chunks):
        rows = []
        for s in range(sets):
            start = pl.multiple_of(chunk * 1024 + own, 512)
            mine = taps[s, :, pl.ds(start, 512)].astype(f32)
            theirs = received[s, :, chunk * 512 : (chunk + 1) * 512].astype(f32)
            rows.append(jnp.where(first, mine, theirs))
            rows.append(jnp.where(first, theirs, mine))
        block = jnp.concatenate(rows, axis=0).astype(bf16)
        for copy in range(copies):
            out[copy * chunks + chunk] = block


def join_own_kernel(core, taps, weight, out):
    out[0] = dot(taps[0], weight[0]) + dot(taps[1], weight[1])
    out[1] = dot(taps[2], weight[2])


def join_other_kernel(core, taps, weight, begun, side, constant, out):
    fixed = begun[0] + dot(taps[0], weight[0]) + dot(taps[1], weight[1])
    constant[...] = fixed
    out[:, :, :512] = to_blocks(fixed + begun[1] + dot(taps[2], weight[2]))
    out[:, :, 512:] = jnp.broadcast_to(side[...], (64, 8, LANES)).astype(bf16)


def both_halves(core, mine, theirs, weight):
    return dot(mine[...], weight[half_rows(core[0])]) + dot(
        theirs[...], weight[half_rows(1 - core[0])]
    )


def join_second_kernel(core, mine, theirs, weight, head, constant, out):
    joined = constant[...] + both_halves(core, mine, theirs, weight.at[0])
    out[:, :, :512] = to_blocks(joined)
    out[:, :, 512:] = to_blocks(both_halves(core, mine, theirs, head))


def logits_kernel(core, mine, theirs, head, out):
    out[...] = to_blocks(both_halves(core, mine, theirs, head))


def head_back_kernel(core, grads, head, *rest):
    *added, out = rest
    value = contract_last(grads[...], head[half_rows(core[0])])
    if added:
        value += added[0][...].astype(f32).reshape(512, 512)
    out[...] = to_blocks(value)


def feed_back_kernel(core, got, weight, head, *rest):
    *added, out = rest
    rows = half_rows(core[0])
    value = contract_last(got[:, :512], weight[0, rows])
    value += contract_last(got[:, 512:], head[rows])
    if added:
        value += added[0][...].astype(f32).reshape(512, 512)
    out[...] = to_blocks(value)


def first_rows_kernel(got, joining, gain, counts, squares):
    terms = []
    for chunk in range(CHUNKS):
        value = column_sum(got, chunk, 0, 512)
        joining[chunk] = value
        terms.append(value * value)
        side = total_over(got, [chunk * CHUNKS, chunk * CHUNKS + 1], 512, 640)
        row = jnp.concatenate([side[i : i + 1] for i in range(4)], axis=1)
        gain[chunk] = jnp.broadcast_to(row, (8, 512))
    squares[...] = lane_total(terms)
    counts[...] = jnp.broadcast_to(column_sum(got, 0, 512, 640)[4:5], (8, LANES))


def second_rows_kernel(got, joining, logits, squares):
    terms = []
    for chunk in range(CHUNKS):
        value = column_sum(got, chunk, 0, 512)
        joining[chunk] = value
        terms.append(value * value)
        logits[chunk] = column_sum(got, chunk, 512, 1536)
    squares[...] = lane_total(terms)


def norm_kernel(joining, gain, squares, squares_other, inverse, out):
    factor = lax.rsqrt((squares[...] + squares_other[...]) / D + norm_eps)
    inverse[...] = factor
    for chunk in range(CHUNKS):
        hidden = (joining[chunk] * factor[:, 0:1] * gain[chunk]).astype(bf16)
        for copy in range(CHUNKS):
            out[copy * CHUNKS + chunk] = hidden


def norm_inner_kernel(got, joining, gain, scaled, inner):
    terms = []
    for chunk in range(CHUNKS):
        value = row_sum(got, chunk, 0, 512) * gain[chunk]
        scaled[chunk] = value
        terms.append(value * joining[chunk])
    inner[...] = lane_total(terms)


def norm_back_kernel(scaled, joining, inverse, inner, inner_other, *rest):
    *riders, out = rest
    factor = inverse[:, 0:1]
    pull = factor * factor * factor * (inner[:, 0:1] + inner_other[:, 0:1]) / D
    for chunk in range(CHUNKS):
        grad = (factor * scaled[chunk] - pull * joining[chunk]).astype(bf16)
        for copy in range(CHUNKS):
            out[chunk * CHUNKS + copy, :, :512] = grad
            if riders:
                out[chunk * CHUNKS + copy, :, 512:] = riders[0][chunk]


def vocab_of(core, chunk):
    return lax.broadcasted_iota(jnp.int32, (8, 1024), 1) + (2 * chunk + core) * 1024


def own_tokens(places, values):
    wide = values.astype(f32)
    lane = lax.broadcasted_iota(jnp.int32, wide.shape, 1)
    return jnp.concatenate(
        [
            jnp.sum(jnp.where(lane == places[1] + i, wide, 0.0), -1, keepdims=True)
            for i in range(2)
        ],
        axis=0,
    )


def stats_kernel(places, got, logits_first, targets, logits_second, stats):
    for chunk in range(CHUNKS):
        logits_second[chunk] = column_sum(got, chunk, 0, 1024)
    columns = []
    for step, logits in enumerate((logits_first, logits_second)):
        top = logits[0]
        for chunk in range(1, CHUNKS):
            top = jnp.maximum(top, logits[chunk])
        top = jnp.max(top, -1, keepdims=True)
        weights = jnp.zeros((8, 1024), f32)
        target = own_tokens(places, targets[step]).astype(jnp.int32)
        picked = jnp.zeros((8, 1024), f32)
        for chunk in range(CHUNKS):
            weights += jnp.exp(logits[chunk] - top)
            hit = vocab_of(places[0], chunk) == target
            picked += jnp.where(hit, logits[chunk], 0.0)
        columns += [
            top,
            jnp.sum(weights, -1, keepdims=True),
            jnp.sum(picked, -1, keepdims=True),
        ]
    stats[...] = put_lanes(8, columns)


def logit_grad_kernel(
    places, stats, stats_other, logits_first, logits_second, targets, masks, counts,
    grads_first, grads_second, loss,
):
    lost = jnp.zeros((8, 1), f32)
    for step, logits in enumerate((logits_first, logits_second)):
        place = 3 * step
        top_mine, top_other = [x[:, place : place + 1] for x in (stats, stats_other)]
        sum_mine, sum_other = [
            x[:, place + 1 : place + 2] for x in (stats, stats_other)
        ]
        picked = stats[:, place + 2 : place + 3] + stats_other[:, place + 2 : place + 3]
        top = jnp.maximum(top_mine, top_other)
        total = sum_mine * jnp.exp(top_mine - top) + sum_other * jnp.exp(top_other - top)
        log_total = top + jnp.log(total)
        weight = own_tokens(places, masks[step]) / counts[:, step : step + 1]
        target = own_tokens(places, targets[step]).astype(jnp.int32)
        lost += weight * (log_total - picked)
        for chunk in range(CHUNKS):
            probs = jnp.exp(logits[chunk] - log_total)
            hit = jnp.where(vocab_of(places[0], chunk) == target, 1.0, 0.0)
            grad = (weight * (probs - hit)).astype(bf16)
            if step == 0:
                grads_first[chunk] = grad
            else:
                for copy in range(CHUNKS):
                    grads_second[chunk * CHUNKS + copy] = grad
    once = jnp.where(places[0] == 0, 1.0, 0.0)
    loss[...] = jnp.broadcast_to(jnp.sum(lost, 0, keepdims=True) * once, (8, LANES))


def grad_kernel(
    core, own, other, mine, theirs, first, second, loss, grad, payload, squares
):
    tap = pl.program_id(0)

    def both(lefts):
        for half, (left, left_later) in enumerate(lefts):
            value = contract_first(left, first[...]) + contract_first(
                left_later, second[...]
            )
            grad[0, half_rows(core[0] if half == 0 else 1 - core[0])] = value
            total = jnp.sum((value * value).reshape(-1, 8, 512), 0)
            total = total[:, :128] + total[:, 128:256] + total[:, 256:384] + total[:, 384:]
            squares[...] += total

    @pl.when(tap == 0)
    def _():
        squares[...] = jnp.zeros((8, LANES), f32)

    @pl.when(tap < 2)
    def _():
        both([(own[0], own[0]), (other[0], other[0])])

    @pl.when(tap == 2)
    def _():
        both([(own[0], mine[...]), (other[0], theirs[...])])
        row = jnp.sum(squares[...], 0, keepdims=True)
        total = jnp.sum(row, -1, keepdims=True)
        lane = lax.broadcasted_iota(jnp.int32, (1, LANES), 1)
        value = jnp.where(lane == 0, total, loss[0:1])
        payload[...] = jnp.broadcast_to(value[None], payload.shape)


def gradients(core, own, other, mine, theirs, first, got, loss):
    tap = lambda s, core: (s, 0, 0)
    still = pl.BlockSpec((512, 512), lambda s, core: (0, 0))
    return pl.pallas_call(
        grad_kernel,
        grid_spec=pltpu.PrefetchScalarGridSpec(
            num_scalar_prefetch=1,
            grid=(3,),
            in_specs=[
                pl.BlockSpec((1, 512, 512), tap),
                pl.BlockSpec((1, 512, 512), tap),
                still,
                still,
                still,
                still,
                pl.BlockSpec((8, LANES), lambda s, core: (0, 0)),
            ],
            out_specs=[
                pl.BlockSpec((1, 1024, 512), tap),
                pl.BlockSpec((128, 1, LANES), lambda s, core: (0, 0, 0)),
            ],
            scratch_shapes=[pltpu.VMEM((8, LANES), f32)],
        ),
        out_shape=[
            jax.ShapeDtypeStruct((3, 1024, 512), f32),
            jax.ShapeDtypeStruct((128, 1, LANES), f32),
        ],
        compiler_params=pltpu.CompilerParams(vmem_limit_bytes=24 * 2**20),
        cost_estimate=pl.CostEstimate(
            flops=6 * 4 * 512 * 512 * 512, bytes_accessed=10 * 2**20, transcendentals=0
        ),
        name="gradients",
    )(core, own, other, mine, theirs, first, got, loss)


def spread_scales(scales):
    terms = []
    for _ in range(3):
        term = scales.astype(bf16)
        terms.append(term.astype(f32))
        scales = scales - terms[-1]
    left = jnp.concatenate(terms + [jnp.zeros((2, scales.shape[1]), f32)], 0).astype(bf16)
    place = lax.broadcasted_iota(jnp.int32, (8, 512), 0) % 2
    block = lax.broadcasted_iota(jnp.int32, (8, 512), 1) // BLOCK
    return contract_first(left, jnp.where(place == block, 1.0, 0.0).astype(bf16))


def adam_kernel(
    shared, weight, grad, first, second, first_scale, second_scale,
    new_weight, new_first, new_second, new_first_scale, new_second_scale, loss,
):
    rows = weight.shape[1]
    total = jnp.sum(shared[:, 0, :], 0, keepdims=True)
    loss[...] = total[:, 1:2]
    clip = jnp.minimum(1.0, clip_norm / (jnp.sqrt(total[:, 0:1]) + 1e-06))
    tap = pl.program_id(0)
    here = pl.ds(pl.multiple_of(pl.program_id(1) * rows, rows), rows)
    old_first = spread_scales(first_scale[tap, :, here] * beta_first)
    old_second = spread_scales(second_scale[tap, :, here] * beta_second)
    new_columns = []
    for block in range(2):
        span = slice(block * BLOCK, (block + 1) * BLOCK)
        clipped = grad[0, :, span] * clip
        first_new = (
            first[0, :, span].astype(f32) * old_first[:, span]
            + (1.0 - beta_first) * clipped
        )
        second_new = (
            second[0, :, span].astype(f32) * old_second[:, span]
            + (1.0 - beta_second) * clipped * clipped
        )
        current = weight[0, :, span].astype(f32)
        spread_sq = second_new * (1.0 / (1.0 - beta_second**step_count))
        spread = spread_sq * lax.rsqrt(spread_sq) + adam_eps
        turned = pl.reciprocal(spread, approx=True)
        turned = turned * (2.0 - spread * turned)
        step = first_new * turned * (learn_rate / (1.0 - beta_first**step_count))
        new_weight[0, :, span] = (
            current * (1.0 - learn_rate * weight_decay) - step
        ).astype(bf16)
        first_top = jnp.max(jnp.abs(first_new), -1, keepdims=True) + scale_eps
        second_top = jnp.max(jnp.abs(second_new), -1, keepdims=True) + scale_eps
        new_first[0, :, span] = (first_new * (1.0 / first_top)).astype(bf16)
        new_second[0, :, span] = (second_new * (1.0 / second_top)).astype(bf16)
        new_columns.append((first_top, second_top))
    lane = lax.broadcasted_iota(jnp.int32, (rows, LANES), 1)
    table = jnp.zeros((rows, LANES), f32)
    for block, (first_top, second_top) in enumerate(new_columns):
        table = jnp.where(lane == block, first_top, table)
        table = jnp.where(lane == 2 + block, second_top, table)
    turned = table.T
    new_first_scale[tap, :, here] = turned[0:2]
    new_second_scale[tap, :, here] = turned[2:4]


def adam(shared, weight, grad, first, second, first_scale, second_scale):
    rows = 512
    wide = pl.BlockSpec((1, rows, 512), lambda s, i: (s, i, 0))
    thin = pl.BlockSpec((3, 2, 1024), lambda s, i: (0, 0, 0))
    return pl.pallas_call(
        adam_kernel,
        grid=(3, 1024 // rows),
        in_specs=[
            pl.BlockSpec((128, 1, LANES), lambda s, i: (0, 0, 0)),
            wide, wide, wide, wide, thin, thin,
        ],
        out_specs=[
            wide, wide, wide, thin, thin, pl.BlockSpec((1, 1), lambda s, i: (0, 0))
        ],
        out_shape=[
            jax.ShapeDtypeStruct((3, 1024, 512), bf16),
            jax.ShapeDtypeStruct((3, 1024, 512), bf16),
            jax.ShapeDtypeStruct((3, 1024, 512), bf16),
            jax.ShapeDtypeStruct((3, 2, 1024), f32),
            jax.ShapeDtypeStruct((3, 2, 1024), f32),
            jax.ShapeDtypeStruct((1, 1), f32),
        ],
        compiler_params=pltpu.CompilerParams(vmem_limit_bytes=34 * 2**20),
        name="update",
    )(shared, weight, grad, first, second, first_scale, second_scale)


def shards(
    taps, gain, join_weight, head_weight, targets, masks,
    first_codes, first_scales, second_codes, second_scales,
):
    core = lax.axis_index("b")
    row = lax.axis_index("p")
    column = lax.axis_index("m")
    own = jnp.stack([core, 2 * row]).astype(jnp.int32)
    other = jnp.stack([1 - core, 2 * row]).astype(jnp.int32)
    chips = ("p", "m")

    def swap(value):
        return lax.ppermute(value, "b", [(0, 1), (1, 0)])

    def exchange(value, axes=chips):
        return lax.all_to_all(value, axes, 0, 0, tiled=False)

    target_ids = jnp.swapaxes(targets, 1, 2)
    mask_ids = jnp.swapaxes(masks, 1, 2)
    gain_rows = gain.reshape(4, LANES)
    gain_high = lax.reduce_precision(gain_rows, 8, 7)
    live = jnp.sum(masks.astype(f32), axis=(1, 2)).reshape(1, STEPS)
    side = jnp.concatenate(
        [
            jnp.where(column % 2 == 0, gain_high, gain_rows - gain_high),
            jnp.pad(live, ((0, 3), (0, LANES - STEPS))),
        ]
    )
    rows_f32, table = ((CHUNKS, 8, 512), f32), ((8, LANES), f32)
    vocab_f32 = ((CHUNKS, 8, 1024), f32)
    blocks = ((64, 8, 512), bf16)
    half_flops = 2 * 512**3
    last_join = pl.BlockSpec((1, 1024, 512), lambda i, core: (2, 0, 0))
    tokens_half, tokens_wide = whole_block((512, 512)), whole_block((512, 1024))
    head_block, parts_block = whole_block((1024, 1024)), whole_block((64, 8, 512))

    with jax.named_scope("taps_in"):
        outgoing = call(
            half_out_kernel, "half_out", [((3, 4, D // 2), bf16)], ("s", own), ("v", taps)
        )
        packed = call(
            half_join_kernel, "half_join", [((64, 24, 512), bf16)],
            ("s", own), ("v", taps), ("v", swap(outgoing)),
        )
        landed = exchange(packed)
        taps_own = landed.reshape(64, 3, 8, 512).transpose(1, 0, 2, 3).reshape(3, 512, 512)
        taps_other = swap(taps_own)

    with jax.named_scope("join_first"):
        sets = whole_block((3, 512, 512))
        begun = call(
            join_own_kernel, "join_own", [((2, 512, 512), f32)],
            ("s", own), ("v", taps_own), ("v", join_weight),
            specs=[sets, pl.BlockSpec((3, 512, 512), lambda i, core: (0, core[0], 0))],
            flops=3 * half_flops,
        )
        constant, parts = call(
            join_other_kernel, "join_other",
            [((512, 512), f32), ((64, 8, 640), bf16)],
            ("s", other), ("v", taps_other), ("v", join_weight), ("v", begun), ("v", side),
            specs=[
                sets,
                pl.BlockSpec((3, 512, 512), lambda i, core: (0, core[0], 0)),
                whole_block((2, 512, 512)),
                whole_block((8, LANES)),
            ],
            flops=3 * half_flops,
        )
        joining_first, gains, counts, squares = call(
            first_rows_kernel, "first_rows", [rows_f32, rows_f32, table, table],
            ("v", exchange(parts)),
        )

    def to_hidden(joining, squares):
        inverse, copies = call(
            norm_kernel, "norm", [table, blocks],
            ("v", joining), ("v", gains), ("v", squares), ("v", swap(squares)),
        )
        mine = exchange(copies).reshape(512, 512)
        return inverse, mine, swap(mine)

    with jax.named_scope("hidden_first"):
        inverse_first, hidden_mine, hidden_theirs = to_hidden(joining_first, squares)

    with jax.named_scope("join_second"):
        parts = call(
            join_second_kernel, "join_second", [((64, 8, 1536), bf16)],
            ("s", own), ("v", hidden_mine), ("v", hidden_theirs), ("v", join_weight),
            ("v", head_weight), ("v", constant),
            specs=[tokens_half, tokens_half, last_join, head_block, tokens_half],
            flops=6 * half_flops,
        )
        joining_second, logits_first, squares = call(
            second_rows_kernel, "second_rows", [rows_f32, vocab_f32, table],
            ("v", exchange(parts)),
        )

    with jax.named_scope("hidden_second"):
        inverse_second, later_mine, later_theirs = to_hidden(joining_second, squares)

    with jax.named_scope("logits"):
        parts = call(
            logits_kernel, "logits", [((64, 8, 1024), bf16)],
            ("s", own), ("v", later_mine), ("v", later_theirs), ("v", head_weight),
            specs=[tokens_half, tokens_half, head_block],
            flops=4 * half_flops,
        )
        got = exchange(parts)

    with jax.named_scope("softmax"):
        logits_second, stats = call(
            stats_kernel, "stats", [vocab_f32, table],
            ("s", own), ("v", got), ("v", logits_first), ("v", target_ids),
        )
        grads_first, copies, loss = call(
            logit_grad_kernel, "logit_grad",
            [((CHUNKS, 8, 1024), bf16), ((64, 8, 1024), bf16), table],
            ("s", own), ("v", stats), ("v", swap(stats)), ("v", logits_first),
            ("v", logits_second), ("v", target_ids), ("v", mask_ids), ("v", counts),
            specs=[
                whole_block((8, LANES)), whole_block((8, LANES)),
                whole_block((CHUNKS, 8, 1024)), whole_block((CHUNKS, 8, 1024)),
                whole_block((STEPS, 4, 16)), whole_block((STEPS, 4, 16)),
                whole_block((8, LANES)),
            ],
        )
        grads_second = exchange(copies).reshape(512, 1024)

    def row_gradients(parts, joining, inverse, *riders):
        scaled, inner = call(
            norm_inner_kernel, "norm_inner", [rows_f32, table],
            ("v", exchange(parts)), ("v", joining), ("v", gains),
        )
        width = 512 + sum(rider.shape[-1] for rider in riders)
        copies = call(
            norm_back_kernel, "norm_back", [((64, 8, width), bf16)],
            ("v", scaled), ("v", joining), ("v", inverse), ("v", inner),
            ("v", swap(inner)), *[("v", rider) for rider in riders],
        )
        return exchange(copies).reshape(512, width)

    with jax.named_scope("back_second"):
        specs, operands = [tokens_wide, head_block], (("v", grads_second), ("v", head_weight))
        away = call(
            head_back_kernel, "head_away", [blocks], ("s", other), *operands,
            specs=specs, flops=2 * half_flops,
        )
        parts = call(
            head_back_kernel, "head_keep", [blocks], ("s", own), *operands,
            ("v", swap(away)), specs=specs + [parts_block], flops=2 * half_flops,
        )
        got = row_gradients(parts, joining_second, inverse_second, grads_first)

    with jax.named_scope("back_first"):
        specs = [whole_block((512, 1536)), last_join, head_block]
        operands = (("v", got), ("v", join_weight), ("v", head_weight))
        away = call(
            feed_back_kernel, "feed_away", [blocks], ("s", other), *operands,
            specs=specs, flops=3 * half_flops,
        )
        parts = call(
            feed_back_kernel, "feed_keep", [blocks], ("s", own), *operands,
            ("v", swap(away)), specs=specs + [parts_block], flops=3 * half_flops,
        )
        first_all = row_gradients(parts, joining_first, inverse_first)

    with jax.named_scope("gradients"):
        grads, payload = gradients(
            own, taps_own, taps_other, hidden_mine, hidden_theirs, first_all, got, loss
        )
        shared = exchange(payload, AXES)

    with jax.named_scope("update"):
        new_join, new_first, new_second, first_scale, second_scale, loss = adam(
            shared,
            join_weight,
            grads,
            first_codes,
            second_codes,
            jnp.swapaxes(first_scales, 1, 2),
            jnp.swapaxes(second_scales, 1, 2),
        )
    return (
        new_join,
        new_first,
        jnp.swapaxes(first_scale, 1, 2),
        new_second,
        jnp.swapaxes(second_scale, 1, 2),
        loss.reshape(()),
    )


def solution(mesh):
    rows = mesh.shape["dp"] // 2
    fine = Mesh(mesh.devices.reshape(rows, 2, mesh.shape["mp"]), AXES)
    dp, mp = ("p", "b"), "m"
    return jax.shard_map(
        shards,
        mesh=fine,
        in_specs=(
            P(None, ("p", "b", "m"), None),
            P(dp),
            P(None, mp, dp),
            P(mp, dp),
            P(None, None, mp),
            P(None, None, mp),
            P(None, mp, dp),
            P(None, mp, dp),
            P(None, mp, dp),
            P(None, mp, dp),
        ),
        out_specs=(
            P(None, mp, dp),
            P(None, mp, dp),
            P(None, mp, dp),
            P(None, mp, dp),
            P(None, mp, dp),
            P(),
        ),
        check_vma=False,
    )
```

```python
import jax
import jax.numpy as jnp
from jax import lax
from jax.experimental import pallas as pl
from jax.experimental.pallas import tpu as pltpu
from jax.sharding import Mesh, PartitionSpec as P

D = 8192
STEPS = 2
BLOCK = 256
LANES = 128
CHUNKS = 8

norm_eps = 1e-05
clip_norm = 1.0
learn_rate = 0.0003
weight_decay = 0.1
beta_first = 0.9
beta_second = 0.999
step_count = 10.0
adam_eps = 1e-08
scale_eps = 1e-12

bf16 = jnp.bfloat16
f32 = jnp.float32
AXES = ("p", "b", "m")
VMEM = pl.BlockSpec(memory_space=pltpu.VMEM)
SMEM = pl.BlockSpec(memory_space=pltpu.SMEM)


def dot(left, right):
    return jnp.dot(left, right, preferred_element_type=f32)


def contract_last(left, right):
    return lax.dot_general(
        left, right, (((1,), (1,)), ((), ())), preferred_element_type=f32
    )


def contract_first(left, right):
    return lax.dot_general(
        left, right, (((0,), (0,)), ((), ())), preferred_element_type=f32
    )


def put_lanes(rows, columns):
    lane = lax.broadcasted_iota(jnp.int32, (rows, LANES), 1)
    block = jnp.zeros((rows, LANES), f32)
    for place, column in enumerate(columns):
        block = jnp.where(lane == place, column, block)
    return block


def total_over(parts, picks, start, stop):
    total = parts[picks[0], :, start:stop].astype(f32)
    for pick in picks[1:]:
        total += parts[pick, :, start:stop].astype(f32)
    return total


def column_sum(parts, row, start, stop):
    return total_over(parts, [row * CHUNKS + m for m in range(CHUNKS)], start, stop)


def row_sum(parts, column, start, stop):
    return total_over(parts, [p * CHUNKS + column for p in range(CHUNKS)], start, stop)


def lane_total(values):
    total = values[0]
    for value in values[1:]:
        total = total + value
    return jnp.broadcast_to(jnp.sum(total, -1, keepdims=True), (8, LANES))


def to_blocks(value):
    return value.reshape(64, 8, value.shape[-1]).astype(bf16)


def half_rows(core):
    return pl.ds(pl.multiple_of(core * 512, 512), 512)


def call(kernel, name, outs, *operands, specs=None, flops=0):
    options = {}
    if specs is None:
        options["in_specs"] = [SMEM if space == "s" else VMEM for space, _ in operands]
        options["out_specs"] = [VMEM] * len(outs)
    else:
        options["grid_spec"] = pltpu.PrefetchScalarGridSpec(
            num_scalar_prefetch=1,
            grid=(1,),
            in_specs=specs,
            out_specs=[whole_block(shape) for shape, _ in outs],
        )
    result = pl.pallas_call(
        kernel,
        out_shape=[jax.ShapeDtypeStruct(shape, dtype) for shape, dtype in outs],
        compiler_params=pltpu.CompilerParams(vmem_limit_bytes=24 * 2**20),
        cost_estimate=pl.CostEstimate(
            flops=flops, bytes_accessed=4 * 2**20, transcendentals=0
        ),
        name=name,
        **options,
    )(*[operand for _, operand in operands])
    return result[0] if len(outs) == 1 else result


def whole_block(shape):
    return pl.BlockSpec(shape, lambda i, core: (0,) * len(shape))


def half_out_kernel(group, taps, out):
    sets, _, width = taps.shape
    chunks = width // 1024
    other = (1 - group[0] % 2) * 512
    for s in range(sets):
        for chunk in range(chunks):
            start = pl.multiple_of(chunk * 1024 + other, 512)
            out[s, :, chunk * 512 : (chunk + 1) * 512] = taps[s, :, pl.ds(start, 512)]


def half_join_kernel(core, taps, received, out):
    sets, _, width = taps.shape
    chunks = width // 1024
    copies = out.shape[0] // chunks
    own = core[0] * 512
    first = core[0] == 0
    for chunk in range(chunks):
        rows = []
        for s in range(sets):
            start = pl.multiple_of(chunk * 1024 + own, 512)
            mine = taps[s, :, pl.ds(start, 512)].astype(f32)
            theirs = received[s, :, chunk * 512 : (chunk + 1) * 512].astype(f32)
            rows.append(jnp.where(first, mine, theirs))
            rows.append(jnp.where(first, theirs, mine))
        block = jnp.concatenate(rows, axis=0).astype(bf16)
        for copy in range(copies):
            out[copy * chunks + chunk] = block


def join_own_kernel(core, taps, weight, out):
    rows = half_rows(core[0])
    out[0] = dot(taps[0], weight[0, rows]) + dot(taps[1], weight[1, rows])
    out[1] = dot(taps[2], weight[2, rows])


def join_other_kernel(core, taps, weight, begun, side, constant, out):
    rows = half_rows(core[0])
    fixed = begun[0] + dot(taps[0], weight[0, rows]) + dot(taps[1], weight[1, rows])
    constant[...] = fixed
    out[:, :, :512] = to_blocks(fixed + begun[1] + dot(taps[2], weight[2, rows]))
    out[:, :, 512:] = jnp.broadcast_to(side[...], (64, 8, LANES)).astype(bf16)


def both_halves(core, mine, theirs, weight):
    return dot(mine[...], weight[half_rows(core[0])]) + dot(
        theirs[...], weight[half_rows(1 - core[0])]
    )


def join_second_kernel(core, mine, theirs, weight, head, constant, out):
    joined = constant[...] + both_halves(core, mine, theirs, weight.at[2])
    out[:, :, :512] = to_blocks(joined)
    out[:, :, 512:] = to_blocks(both_halves(core, mine, theirs, head))


def logits_kernel(core, mine, theirs, head, out):
    out[...] = to_blocks(both_halves(core, mine, theirs, head))


def head_back_kernel(core, grads, head, *rest):
    *added, out = rest
    value = contract_last(grads[...], head[half_rows(core[0])])
    if added:
        value += added[0][...].astype(f32).reshape(512, 512)
    out[...] = to_blocks(value)


def feed_back_kernel(core, got, weight, head, *rest):
    *added, out = rest
    rows = half_rows(core[0])
    value = contract_last(got[:, :512], weight[2, rows])
    value += contract_last(got[:, 512:], head[rows])
    if added:
        value += added[0][...].astype(f32).reshape(512, 512)
    out[...] = to_blocks(value)


def first_rows_kernel(got, joining, gain, counts, squares):
    terms = []
    for chunk in range(CHUNKS):
        value = column_sum(got, chunk, 0, 512)
        joining[chunk] = value
        terms.append(value * value)
        side = total_over(got, [chunk * CHUNKS, chunk * CHUNKS + 1], 512, 640)
        row = jnp.concatenate([side[i : i + 1] for i in range(4)], axis=1)
        gain[chunk] = jnp.broadcast_to(row, (8, 512))
    squares[...] = lane_total(terms)
    counts[...] = jnp.broadcast_to(column_sum(got, 0, 512, 640)[4:5], (8, LANES))


def second_rows_kernel(got, joining, logits, squares):
    terms = []
    for chunk in range(CHUNKS):
        value = column_sum(got, chunk, 0, 512)
        joining[chunk] = value
        terms.append(value * value)
        logits[chunk] = column_sum(got, chunk, 512, 1536)
    squares[...] = lane_total(terms)


def norm_kernel(joining, gain, squares, squares_other, inverse, out):
    factor = lax.rsqrt((squares[...] + squares_other[...]) / D + norm_eps)
    inverse[...] = factor
    for chunk in range(CHUNKS):
        hidden = (joining[chunk] * factor[:, 0:1] * gain[chunk]).astype(bf16)
        for copy in range(CHUNKS):
            out[copy * CHUNKS + chunk] = hidden


def norm_inner_kernel(got, joining, gain, scaled, inner):
    terms = []
    for chunk in range(CHUNKS):
        value = row_sum(got, chunk, 0, 512) * gain[chunk]
        scaled[chunk] = value
        terms.append(value * joining[chunk])
    inner[...] = lane_total(terms)


def norm_back_kernel(scaled, joining, inverse, inner, inner_other, *rest):
    *riders, out = rest
    factor = inverse[:, 0:1]
    pull = factor * factor * factor * (inner[:, 0:1] + inner_other[:, 0:1]) / D
    for chunk in range(CHUNKS):
        grad = (factor * scaled[chunk] - pull * joining[chunk]).astype(bf16)
        for copy in range(CHUNKS):
            out[chunk * CHUNKS + copy, :, :512] = grad
            if riders:
                out[chunk * CHUNKS + copy, :, 512:] = riders[0][chunk]


def vocab_of(core, chunk):
    return lax.broadcasted_iota(jnp.int32, (8, 1024), 1) + (2 * chunk + core) * 1024


def own_tokens(group, values):
    wide = values.astype(f32)
    lane = lax.broadcasted_iota(jnp.int32, wide.shape, 1)
    return jnp.concatenate(
        [
            jnp.sum(jnp.where(lane == group[0] - group[0] % 2 + i, wide, 0.0), -1, keepdims=True)
            for i in range(2)
        ],
        axis=0,
    )


def stats_kernel(group, got, logits_first, targets, logits_second, stats):
    for chunk in range(CHUNKS):
        logits_second[chunk] = column_sum(got, chunk, 0, 1024)
    columns = []
    for step, logits in enumerate((logits_first, logits_second)):
        top = logits[0]
        for chunk in range(1, CHUNKS):
            top = jnp.maximum(top, logits[chunk])
        top = jnp.max(top, -1, keepdims=True)
        weights = jnp.zeros((8, 1024), f32)
        target = own_tokens(group, targets[step]).astype(jnp.int32)
        picked = jnp.zeros((8, 1024), f32)
        for chunk in range(CHUNKS):
            weights += jnp.exp(logits[chunk] - top)
            hit = vocab_of(group[0] % 2, chunk) == target
            picked += jnp.where(hit, logits[chunk], 0.0)
        columns += [
            top,
            jnp.sum(weights, -1, keepdims=True),
            jnp.sum(picked, -1, keepdims=True),
        ]
    stats[...] = put_lanes(8, columns)


def logit_grad_kernel(
    group, stats, stats_other, logits_first, logits_second, targets, masks, counts,
    grads_first, grads_second, loss,
):
    lost = jnp.zeros((8, 1), f32)
    for step, logits in enumerate((logits_first, logits_second)):
        place = 3 * step
        top_mine, top_other = [x[:, place : place + 1] for x in (stats, stats_other)]
        sum_mine, sum_other = [
            x[:, place + 1 : place + 2] for x in (stats, stats_other)
        ]
        picked = stats[:, place + 2 : place + 3] + stats_other[:, place + 2 : place + 3]
        top = jnp.maximum(top_mine, top_other)
        total = sum_mine * jnp.exp(top_mine - top) + sum_other * jnp.exp(top_other - top)
        log_total = top + jnp.log(total)
        weight = own_tokens(group, masks[step]) / counts[:, step : step + 1]
        target = own_tokens(group, targets[step]).astype(jnp.int32)
        lost += weight * (log_total - picked)
        for chunk in range(CHUNKS):
            probs = jnp.exp(logits[chunk] - log_total)
            hit = jnp.where(vocab_of(group[0] % 2, chunk) == target, 1.0, 0.0)
            grad = (weight * (probs - hit)).astype(bf16)
            if step == 0:
                grads_first[chunk] = grad
            else:
                for copy in range(CHUNKS):
                    grads_second[chunk * CHUNKS + copy] = grad
    once = jnp.where(group[0] % 2 == 0, 1.0, 0.0)
    loss[...] = jnp.broadcast_to(jnp.sum(lost, 0, keepdims=True) * once, (8, LANES))


def grad_kernel(
    core, own, other, mine, theirs, first, second, loss, grad, payload, squares
):
    tap = pl.program_id(0)

    def both(lefts):
        for half, (left, left_later) in enumerate(lefts):
            value = contract_first(left, first[...]) + contract_first(
                left_later, second[...]
            )
            grad[0, half_rows(core[0] if half == 0 else 1 - core[0])] = value
            total = jnp.sum((value * value).reshape(-1, 8, 512), 0)
            total = total[:, :128] + total[:, 128:256] + total[:, 256:384] + total[:, 384:]
            squares[...] += total

    @pl.when(tap == 0)
    def _():
        squares[...] = jnp.zeros((8, LANES), f32)

    @pl.when(tap < 2)
    def _():
        both([(own[0], own[0]), (other[0], other[0])])

    @pl.when(tap == 2)
    def _():
        both([(own[0], mine[...]), (other[0], theirs[...])])
        row = jnp.sum(squares[...], 0, keepdims=True)
        total = jnp.sum(row, -1, keepdims=True)
        lane = lax.broadcasted_iota(jnp.int32, (1, LANES), 1)
        value = jnp.where(lane == 0, total, loss[0:1])
        payload[...] = jnp.broadcast_to(value[None], payload.shape)


def gradients(core, own, other, mine, theirs, first, got, loss):
    tap = lambda s, core: (s, 0, 0)
    still = pl.BlockSpec((512, 512), lambda s, core: (0, 0))
    return pl.pallas_call(
        grad_kernel,
        grid_spec=pltpu.PrefetchScalarGridSpec(
            num_scalar_prefetch=1,
            grid=(3,),
            in_specs=[
                pl.BlockSpec((1, 512, 512), tap),
                pl.BlockSpec((1, 512, 512), tap),
                still,
                still,
                still,
                still,
                pl.BlockSpec((8, LANES), lambda s, core: (0, 0)),
            ],
            out_specs=[
                pl.BlockSpec((1, 1024, 512), tap),
                pl.BlockSpec((128, 1, LANES), lambda s, core: (0, 0, 0)),
            ],
            scratch_shapes=[pltpu.VMEM((8, LANES), f32)],
        ),
        out_shape=[
            jax.ShapeDtypeStruct((3, 1024, 512), f32),
            jax.ShapeDtypeStruct((128, 1, LANES), f32),
        ],
        compiler_params=pltpu.CompilerParams(vmem_limit_bytes=24 * 2**20),
        cost_estimate=pl.CostEstimate(
            flops=6 * 4 * 512 * 512 * 512, bytes_accessed=10 * 2**20, transcendentals=0
        ),
        name="gradients",
    )(core, own, other, mine, theirs, first, got, loss)


def spread_scales(scales):
    terms = []
    for _ in range(3):
        term = scales.astype(bf16)
        terms.append(term.astype(f32))
        scales = scales - terms[-1]
    left = jnp.concatenate(terms + [jnp.zeros((2, scales.shape[1]), f32)], 0).astype(bf16)
    place = lax.broadcasted_iota(jnp.int32, (8, 512), 0) % 2
    block = lax.broadcasted_iota(jnp.int32, (8, 512), 1) // BLOCK
    return contract_first(left, jnp.where(place == block, 1.0, 0.0).astype(bf16))


def adam_kernel(
    shared, weight, grad, first, second, first_scale, second_scale,
    new_weight, new_first, new_second, new_first_scale, new_second_scale, loss,
):
    rows = weight.shape[1]
    total = jnp.sum(shared[:, 0, :], 0, keepdims=True)
    loss[...] = total[:, 1:2]
    clip = jnp.minimum(1.0, clip_norm / (jnp.sqrt(total[:, 0:1]) + 1e-06))
    tap = pl.program_id(0)
    here = pl.ds(pl.multiple_of(pl.program_id(1) * rows, rows), rows)
    old_first = spread_scales(first_scale[tap, :, here] * beta_first)
    old_second = spread_scales(second_scale[tap, :, here] * beta_second)
    new_columns = []
    for block in range(2):
        span = slice(block * BLOCK, (block + 1) * BLOCK)
        clipped = grad[0, :, span] * clip
        first_new = (
            first[0, :, span].astype(f32) * old_first[:, span]
            + (1.0 - beta_first) * clipped
        )
        second_new = (
            second[0, :, span].astype(f32) * old_second[:, span]
            + (1.0 - beta_second) * clipped * clipped
        )
        current = weight[0, :, span].astype(f32)
        spread_sq = second_new * (1.0 / (1.0 - beta_second**step_count))
        spread = spread_sq * lax.rsqrt(spread_sq) + adam_eps
        turned = pl.reciprocal(spread, approx=True)
        turned = turned * (2.0 - spread * turned)
        step = first_new * turned * (learn_rate / (1.0 - beta_first**step_count))
        new_weight[0, :, span] = (
            current * (1.0 - learn_rate * weight_decay) - step
        ).astype(bf16)
        first_top = jnp.max(jnp.abs(first_new), -1, keepdims=True) + scale_eps
        second_top = jnp.max(jnp.abs(second_new), -1, keepdims=True) + scale_eps
        new_first[0, :, span] = (first_new * (1.0 / first_top)).astype(bf16)
        new_second[0, :, span] = (second_new * (1.0 / second_top)).astype(bf16)
        new_columns.append((first_top, second_top))
    lane = lax.broadcasted_iota(jnp.int32, (rows, LANES), 1)
    table = jnp.zeros((rows, LANES), f32)
    for block, (first_top, second_top) in enumerate(new_columns):
        table = jnp.where(lane == block, first_top, table)
        table = jnp.where(lane == 2 + block, second_top, table)
    turned = table.T
    new_first_scale[tap, :, here] = turned[0:2]
    new_second_scale[tap, :, here] = turned[2:4]


def adam(shared, weight, grad, first, second, first_scale, second_scale):
    rows = 512
    wide = pl.BlockSpec((1, rows, 512), lambda s, i: (s, i, 0))
    thin = pl.BlockSpec((3, 2, 1024), lambda s, i: (0, 0, 0))
    return pl.pallas_call(
        adam_kernel,
        grid=(3, 1024 // rows),
        in_specs=[
            pl.BlockSpec((128, 1, LANES), lambda s, i: (0, 0, 0)),
            wide, wide, wide, wide, thin, thin,
        ],
        out_specs=[
            wide, wide, wide, thin, thin, pl.BlockSpec((1, 1), lambda s, i: (0, 0))
        ],
        out_shape=[
            jax.ShapeDtypeStruct((3, 1024, 512), bf16),
            jax.ShapeDtypeStruct((3, 1024, 512), bf16),
            jax.ShapeDtypeStruct((3, 1024, 512), bf16),
            jax.ShapeDtypeStruct((3, 2, 1024), f32),
            jax.ShapeDtypeStruct((3, 2, 1024), f32),
            jax.ShapeDtypeStruct((1, 1), f32),
        ],
        compiler_params=pltpu.CompilerParams(vmem_limit_bytes=34 * 2**20),
        name="update",
    )(shared, weight, grad, first, second, first_scale, second_scale)


def shards(
    taps, gain, join_weight, head_weight, targets, masks,
    first_codes, first_scales, second_codes, second_scales,
):
    core = lax.axis_index("b")
    row = lax.axis_index("p")
    column = lax.axis_index("m")
    own = core.reshape(1).astype(jnp.int32)
    other = 1 - own
    group = (2 * row + core).reshape(1).astype(jnp.int32)
    chips = ("p", "m")

    def swap(value):
        return lax.ppermute(value, "b", [(0, 1), (1, 0)])

    def exchange(value, axes=chips):
        return lax.all_to_all(value, axes, 0, 0, tiled=False)

    target_ids = jnp.swapaxes(targets, 1, 2)
    mask_ids = jnp.swapaxes(masks, 1, 2)
    gain_rows = gain.reshape(4, LANES)
    gain_high = lax.reduce_precision(gain_rows, 8, 7)
    live = jnp.sum(masks.astype(f32), axis=(1, 2)).reshape(1, STEPS)
    side = jnp.concatenate(
        [
            jnp.where(column % 2 == 0, gain_high, gain_rows - gain_high),
            jnp.pad(live, ((0, 3), (0, LANES - STEPS))),
        ]
    )
    rows_f32, table = ((CHUNKS, 8, 512), f32), ((8, LANES), f32)
    vocab_f32 = ((CHUNKS, 8, 1024), f32)
    blocks = ((64, 8, 512), bf16)
    half_flops = 2 * 512**3

    with jax.named_scope("taps_in"):
        outgoing = call(
            half_out_kernel, "half_out", [((3, 4, D // 2), bf16)], ("s", group), ("v", taps)
        )
        packed = call(
            half_join_kernel, "half_join", [((64, 24, 512), bf16)],
            ("s", own), ("v", taps), ("v", swap(outgoing)),
        )
        landed = exchange(packed)
        taps_own = landed.reshape(64, 3, 8, 512).transpose(1, 0, 2, 3).reshape(3, 512, 512)
        taps_other = swap(taps_own)

    with jax.named_scope("join_first"):
        begun = call(
            join_own_kernel, "join_own", [((2, 512, 512), f32)],
            ("s", own), ("v", taps_own), ("v", join_weight),
            flops=3 * half_flops,
        )
        constant, parts = call(
            join_other_kernel, "join_other",
            [((512, 512), f32), ((64, 8, 640), bf16)],
            ("s", other), ("v", taps_other), ("v", join_weight), ("v", begun), ("v", side),
            flops=3 * half_flops,
        )
        joining_first, gains, counts, squares = call(
            first_rows_kernel, "first_rows", [rows_f32, rows_f32, table, table],
            ("v", exchange(parts)),
        )

    def to_hidden(joining, squares):
        inverse, copies = call(
            norm_kernel, "norm", [table, blocks],
            ("v", joining), ("v", gains), ("v", squares), ("v", swap(squares)),
        )
        mine = exchange(copies).reshape(512, 512)
        return inverse, mine, swap(mine)

    with jax.named_scope("hidden_first"):
        inverse_first, hidden_mine, hidden_theirs = to_hidden(joining_first, squares)

    with jax.named_scope("join_second"):
        parts = call(
            join_second_kernel, "join_second", [((64, 8, 1536), bf16)],
            ("s", own), ("v", hidden_mine), ("v", hidden_theirs), ("v", join_weight),
            ("v", head_weight), ("v", constant),
            flops=6 * half_flops,
        )
        joining_second, logits_first, squares = call(
            second_rows_kernel, "second_rows", [rows_f32, vocab_f32, table],
            ("v", exchange(parts)),
        )

    with jax.named_scope("hidden_second"):
        inverse_second, later_mine, later_theirs = to_hidden(joining_second, squares)

    with jax.named_scope("logits"):
        parts = call(
            logits_kernel, "logits", [((64, 8, 1024), bf16)],
            ("s", own), ("v", later_mine), ("v", later_theirs), ("v", head_weight),
            flops=4 * half_flops,
        )
        got = exchange(parts)

    with jax.named_scope("softmax"):
        logits_second, stats = call(
            stats_kernel, "stats", [vocab_f32, table],
            ("s", group), ("v", got), ("v", logits_first), ("v", target_ids),
        )
        grads_first, copies, loss = call(
            logit_grad_kernel, "logit_grad",
            [((CHUNKS, 8, 1024), bf16), ((64, 8, 1024), bf16), table],
            ("s", group), ("v", stats), ("v", swap(stats)), ("v", logits_first),
            ("v", logits_second), ("v", target_ids), ("v", mask_ids), ("v", counts),
            specs=[
                whole_block((8, LANES)), whole_block((8, LANES)),
                whole_block((CHUNKS, 8, 1024)), whole_block((CHUNKS, 8, 1024)),
                whole_block((STEPS, 4, 16)), whole_block((STEPS, 4, 16)),
                whole_block((8, LANES)),
            ],
        )
        grads_second = exchange(copies).reshape(512, 1024)

    def row_gradients(parts, joining, inverse, *riders):
        scaled, inner = call(
            norm_inner_kernel, "norm_inner", [rows_f32, table],
            ("v", exchange(parts)), ("v", joining), ("v", gains),
        )
        width = 512 + sum(rider.shape[-1] for rider in riders)
        copies = call(
            norm_back_kernel, "norm_back", [((64, 8, width), bf16)],
            ("v", scaled), ("v", joining), ("v", inverse), ("v", inner),
            ("v", swap(inner)), *[("v", rider) for rider in riders],
        )
        return exchange(copies).reshape(512, width)

    with jax.named_scope("back_second"):
        operands = (("v", grads_second), ("v", head_weight))
        away = call(
            head_back_kernel, "head_away", [blocks], ("s", other), *operands,
            flops=2 * half_flops,
        )
        parts = call(
            head_back_kernel, "head_keep", [blocks], ("s", own), *operands,
            ("v", swap(away)), flops=2 * half_flops,
        )
        got = row_gradients(parts, joining_second, inverse_second, grads_first)

    with jax.named_scope("back_first"):
        operands = (("v", got), ("v", join_weight), ("v", head_weight))
        away = call(
            feed_back_kernel, "feed_away", [blocks], ("s", other), *operands,
            flops=3 * half_flops,
        )
        parts = call(
            feed_back_kernel, "feed_keep", [blocks], ("s", own), *operands,
            ("v", swap(away)), flops=3 * half_flops,
        )
        first_all = row_gradients(parts, joining_first, inverse_first)

    with jax.named_scope("gradients"):
        grads, payload = gradients(
            own, taps_own, taps_other, hidden_mine, hidden_theirs, first_all, got, loss
        )
        shared = exchange(payload, AXES)

    with jax.named_scope("update"):
        new_join, new_first, new_second, first_scale, second_scale, loss = adam(
            shared,
            join_weight,
            grads,
            first_codes,
            second_codes,
            jnp.swapaxes(first_scales, 1, 2),
            jnp.swapaxes(second_scales, 1, 2),
        )
    return (
        new_join,
        new_first,
        jnp.swapaxes(first_scale, 1, 2),
        new_second,
        jnp.swapaxes(second_scale, 1, 2),
        loss.reshape(()),
    )


def solution(mesh):
    rows = mesh.shape["dp"] // 2
    fine = Mesh(mesh.devices.reshape(rows, 2, mesh.shape["mp"]), AXES)
    dp, mp = ("p", "b"), "m"
    return jax.shard_map(
        shards,
        mesh=fine,
        in_specs=(
            P(None, ("p", "b", "m"), None),
            P(dp),
            P(None, mp, dp),
            P(mp, dp),
            P(None, None, mp),
            P(None, None, mp),
            P(None, mp, dp),
            P(None, mp, dp),
            P(None, mp, dp),
            P(None, mp, dp),
        ),
        out_specs=(
            P(None, mp, dp),
            P(None, mp, dp),
            P(None, mp, dp),
            P(None, mp, dp),
            P(None, mp, dp),
            P(),
        ),
        check_vma=False,
    )
```

```python
import jax
import jax.numpy as jnp
from jax import lax
from jax.experimental import pallas as pl
from jax.experimental.pallas import tpu as pltpu
from jax.sharding import Mesh, PartitionSpec as P

D = 8192
STEPS = 2
BLOCK = 256
LANES = 128
CHUNKS = 8

norm_eps = 1e-05
clip_norm = 1.0
learn_rate = 0.0003
weight_decay = 0.1
beta_first = 0.9
beta_second = 0.999
step_count = 10.0
adam_eps = 1e-08
scale_eps = 1e-12

bf16 = jnp.bfloat16
f32 = jnp.float32
AXES = ("p", "b", "m")
VMEM = pl.BlockSpec(memory_space=pltpu.VMEM)
SMEM = pl.BlockSpec(memory_space=pltpu.SMEM)


def dot(left, right):
    return jnp.dot(left, right, preferred_element_type=f32)


def contract_last(left, right):
    return lax.dot_general(
        left, right, (((1,), (1,)), ((), ())), preferred_element_type=f32
    )


def contract_first(left, right):
    return lax.dot_general(
        left, right, (((0,), (0,)), ((), ())), preferred_element_type=f32
    )


def put_lanes(rows, columns):
    lane = lax.broadcasted_iota(jnp.int32, (rows, LANES), 1)
    block = jnp.zeros((rows, LANES), f32)
    for place, column in enumerate(columns):
        block = jnp.where(lane == place, column, block)
    return block


def total_over(parts, picks, start, stop):
    total = parts[picks[0], :, start:stop].astype(f32)
    for pick in picks[1:]:
        total += parts[pick, :, start:stop].astype(f32)
    return total


def column_sum(parts, row, start, stop):
    return total_over(parts, [row * CHUNKS + m for m in range(CHUNKS)], start, stop)


def row_sum(parts, column, start, stop):
    return total_over(parts, [p * CHUNKS + column for p in range(CHUNKS)], start, stop)


def lane_total(values):
    total = values[0]
    for value in values[1:]:
        total = total + value
    return jnp.broadcast_to(jnp.sum(total, -1, keepdims=True), (8, LANES))


def to_blocks(value):
    return value.reshape(64, 8, value.shape[-1]).astype(bf16)


def half_rows(core):
    return pl.ds(pl.multiple_of(core * 512, 512), 512)


def call(kernel, name, outs, *operands, specs=None, flops=0):
    options = {}
    if specs is None:
        options["in_specs"] = [SMEM if space == "s" else VMEM for space, _ in operands]
        options["out_specs"] = [VMEM] * len(outs)
    else:
        options["grid_spec"] = pltpu.PrefetchScalarGridSpec(
            num_scalar_prefetch=1,
            grid=(1,),
            in_specs=specs,
            out_specs=[whole_block(shape) for shape, _ in outs],
        )
    result = pl.pallas_call(
        kernel,
        out_shape=[jax.ShapeDtypeStruct(shape, dtype) for shape, dtype in outs],
        compiler_params=pltpu.CompilerParams(vmem_limit_bytes=24 * 2**20),
        cost_estimate=pl.CostEstimate(
            flops=flops, bytes_accessed=4 * 2**20, transcendentals=0
        ),
        name=name,
        **options,
    )(*[operand for _, operand in operands])
    return result[0] if len(outs) == 1 else result


def whole_block(shape):
    return pl.BlockSpec(shape, lambda i, core: (0,) * len(shape))


def half_out_kernel(group, taps, kept, out):
    sets, _, width = taps.shape
    core = group[0] % 2
    for s in range(sets):
        for chunk in range(width // 1024):
            place = slice(chunk * 512, (chunk + 1) * 512)
            for half, target in ((core, kept), (1 - core, out)):
                start = pl.multiple_of(chunk * 1024 + half * 512, 512)
                target[s, :, place] = taps[s, :, pl.ds(start, 512)]


def half_join_kernel(core, kept, received, out):
    sets, _, width = kept.shape
    chunks = width // 512
    copies = out.shape[0] // chunks
    first = core[0] == 0
    for chunk in range(chunks):
        rows = []
        for s in range(sets):
            mine = kept[s, :, chunk * 512 : (chunk + 1) * 512].astype(f32)
            theirs = received[s, :, chunk * 512 : (chunk + 1) * 512].astype(f32)
            rows.append(jnp.where(first, mine, theirs))
            rows.append(jnp.where(first, theirs, mine))
        block = jnp.concatenate(rows, axis=0).astype(bf16)
        for copy in range(copies):
            out[copy * chunks + chunk] = block


def join_own_kernel(core, taps, weight, out):
    rows = half_rows(core[0])
    out[0] = dot(taps[0], weight[0, rows]) + dot(taps[1], weight[1, rows])
    out[1] = dot(taps[2], weight[2, rows])


def join_other_kernel(core, taps, weight, begun, side, constant, out):
    rows = half_rows(core[0])
    fixed = begun[0] + dot(taps[0], weight[0, rows]) + dot(taps[1], weight[1, rows])
    constant[...] = fixed
    out[:, :, :512] = to_blocks(fixed + begun[1] + dot(taps[2], weight[2, rows]))
    out[:, :, 512:] = jnp.broadcast_to(side[...], (64, 8, LANES)).astype(bf16)


def both_halves(core, mine, theirs, weight):
    return dot(mine[...], weight[half_rows(core[0])]) + dot(
        theirs[...], weight[half_rows(1 - core[0])]
    )


def join_second_kernel(core, mine, theirs, weight, head, constant, out):
    joined = constant[...] + both_halves(core, mine, theirs, weight.at[2])
    out[:, :, :512] = to_blocks(joined)
    out[:, :, 512:] = to_blocks(both_halves(core, mine, theirs, head))


def logits_kernel(core, mine, theirs, head, out):
    out[...] = to_blocks(both_halves(core, mine, theirs, head))


def head_back_kernel(core, grads, head, *rest):
    *added, out = rest
    value = contract_last(grads[...], head[half_rows(core[0])])
    if added:
        value += added[0][...].astype(f32).reshape(512, 512)
    out[...] = to_blocks(value)


def feed_back_kernel(core, got, weight, head, *rest):
    *added, out = rest
    rows = half_rows(core[0])
    value = contract_last(got[:, :512], weight[2, rows])
    value += contract_last(got[:, 512:], head[rows])
    if added:
        value += added[0][...].astype(f32).reshape(512, 512)
    out[...] = to_blocks(value)


def first_rows_kernel(got, joining, gain, counts, squares):
    terms = []
    for chunk in range(CHUNKS):
        value = column_sum(got, chunk, 0, 512)
        joining[chunk] = value
        terms.append(value * value)
        side = total_over(got, [chunk * CHUNKS, chunk * CHUNKS + 1], 512, 640)
        row = jnp.concatenate([side[i : i + 1] for i in range(4)], axis=1)
        gain[chunk] = jnp.broadcast_to(row, (8, 512))
    squares[...] = lane_total(terms)
    counts[...] = jnp.broadcast_to(column_sum(got, 0, 512, 640)[4:5], (8, LANES))


def second_rows_kernel(got, joining, logits, squares):
    terms = []
    for chunk in range(CHUNKS):
        value = column_sum(got, chunk, 0, 512)
        joining[chunk] = value
        terms.append(value * value)
        logits[chunk] = column_sum(got, chunk, 512, 1536)
    squares[...] = lane_total(terms)


def norm_kernel(joining, gain, squares, squares_other, inverse, out):
    factor = lax.rsqrt((squares[...] + squares_other[...]) / D + norm_eps)
    inverse[...] = factor
    for chunk in range(CHUNKS):
        hidden = (joining[chunk] * factor[:, 0:1] * gain[chunk]).astype(bf16)
        for copy in range(CHUNKS):
            out[copy * CHUNKS + chunk] = hidden


def norm_inner_kernel(got, joining, gain, scaled, inner):
    terms = []
    for chunk in range(CHUNKS):
        value = row_sum(got, chunk, 0, 512) * gain[chunk]
        scaled[chunk] = value
        terms.append(value * joining[chunk])
    inner[...] = lane_total(terms)


def norm_back_kernel(scaled, joining, inverse, inner, inner_other, *rest):
    *riders, out = rest
    factor = inverse[:, 0:1]
    pull = factor * factor * factor * (inner[:, 0:1] + inner_other[:, 0:1]) / D
    for chunk in range(CHUNKS):
        grad = (factor * scaled[chunk] - pull * joining[chunk]).astype(bf16)
        for copy in range(CHUNKS):
            out[chunk * CHUNKS + copy, :, :512] = grad
            if riders:
                out[chunk * CHUNKS + copy, :, 512:] = riders[0][chunk]


def vocab_of(core, chunk):
    return lax.broadcasted_iota(jnp.int32, (8, 1024), 1) + (2 * chunk + core) * 1024


def own_tokens(group, values):
    wide = values.astype(f32)
    lane = lax.broadcasted_iota(jnp.int32, wide.shape, 1)
    return jnp.concatenate(
        [
            jnp.sum(jnp.where(lane == group[0] - group[0] % 2 + i, wide, 0.0), -1, keepdims=True)
            for i in range(2)
        ],
        axis=0,
    )


def stats_kernel(group, got, logits_first, targets, logits_second, stats):
    for chunk in range(CHUNKS):
        logits_second[chunk] = column_sum(got, chunk, 0, 1024)
    columns = []
    for step, logits in enumerate((logits_first, logits_second)):
        top = logits[0]
        for chunk in range(1, CHUNKS):
            top = jnp.maximum(top, logits[chunk])
        top = jnp.max(top, -1, keepdims=True)
        weights = jnp.zeros((8, 1024), f32)
        target = own_tokens(group, targets[step]).astype(jnp.int32)
        picked = jnp.zeros((8, 1024), f32)
        for chunk in range(CHUNKS):
            weights += jnp.exp(logits[chunk] - top)
            hit = vocab_of(group[0] % 2, chunk) == target
            picked += jnp.where(hit, logits[chunk], 0.0)
        columns += [
            top,
            jnp.sum(weights, -1, keepdims=True),
            jnp.sum(picked, -1, keepdims=True),
        ]
    stats[...] = put_lanes(8, columns)


def logit_grad_kernel(
    group, stats, stats_other, logits_first, logits_second, targets, masks, counts,
    grads_first, grads_second, loss,
):
    lost = jnp.zeros((8, 1), f32)
    for step, logits in enumerate((logits_first, logits_second)):
        place = 3 * step
        top_mine, top_other = [x[:, place : place + 1] for x in (stats, stats_other)]
        sum_mine, sum_other = [
            x[:, place + 1 : place + 2] for x in (stats, stats_other)
        ]
        picked = stats[:, place + 2 : place + 3] + stats_other[:, place + 2 : place + 3]
        top = jnp.maximum(top_mine, top_other)
        total = sum_mine * jnp.exp(top_mine - top) + sum_other * jnp.exp(top_other - top)
        log_total = top + jnp.log(total)
        weight = own_tokens(group, masks[step]) / counts[:, step : step + 1]
        target = own_tokens(group, targets[step]).astype(jnp.int32)
        lost += weight * (log_total - picked)
        for chunk in range(CHUNKS):
            probs = jnp.exp(logits[chunk] - log_total)
            hit = jnp.where(vocab_of(group[0] % 2, chunk) == target, 1.0, 0.0)
            grad = (weight * (probs - hit)).astype(bf16)
            if step == 0:
                grads_first[chunk] = grad
            else:
                for copy in range(CHUNKS):
                    grads_second[chunk * CHUNKS + copy] = grad
    once = jnp.where(group[0] % 2 == 0, 1.0, 0.0)
    loss[...] = jnp.broadcast_to(jnp.sum(lost, 0, keepdims=True) * once, (8, LANES))


def grad_kernel(
    core, own, other, mine, theirs, first, second, loss, grad, payload, squares, summed
):
    tap = pl.program_id(0)

    def both(values):
        for half, value in enumerate(values):
            grad[0, half_rows(core[0] if half == 0 else 1 - core[0])] = value
            total = jnp.sum((value * value).reshape(-1, 8, 512), 0)
            total = total[:, :128] + total[:, 128:256] + total[:, 256:384] + total[:, 384:]
            squares[...] += total

    @pl.when(tap == 0)
    def _():
        squares[...] = jnp.zeros((8, LANES), f32)
        summed[...] = (first[...].astype(f32) + second[...].astype(f32)).astype(bf16)

    @pl.when(tap < 2)
    def _():
        both([contract_first(left[0], summed[...]) for left in (own, other)])

    @pl.when(tap == 2)
    def _():
        both(
            [
                contract_first(left[0], first[...]) + contract_first(later[...], second[...])
                for left, later in ((own, mine), (other, theirs))
            ]
        )
        row = jnp.sum(squares[...], 0, keepdims=True)
        total = jnp.sum(row, -1, keepdims=True)
        lane = lax.broadcasted_iota(jnp.int32, (1, LANES), 1)
        value = jnp.where(lane == 0, total, loss[0:1])
        payload[...] = jnp.broadcast_to(value[None], payload.shape)


def gradients(core, own, other, mine, theirs, first, got, loss):
    tap = lambda s, core: (s, 0, 0)
    still = pl.BlockSpec((512, 512), lambda s, core: (0, 0))
    return pl.pallas_call(
        grad_kernel,
        grid_spec=pltpu.PrefetchScalarGridSpec(
            num_scalar_prefetch=1,
            grid=(3,),
            in_specs=[
                pl.BlockSpec((1, 512, 512), tap),
                pl.BlockSpec((1, 512, 512), tap),
                still,
                still,
                still,
                still,
                pl.BlockSpec((8, LANES), lambda s, core: (0, 0)),
            ],
            out_specs=[
                pl.BlockSpec((1, 1024, 512), tap),
                pl.BlockSpec((128, 1, LANES), lambda s, core: (0, 0, 0)),
            ],
            scratch_shapes=[pltpu.VMEM((8, LANES), f32), pltpu.VMEM((512, 512), bf16)],
        ),
        out_shape=[
            jax.ShapeDtypeStruct((3, 1024, 512), f32),
            jax.ShapeDtypeStruct((128, 1, LANES), f32),
        ],
        compiler_params=pltpu.CompilerParams(vmem_limit_bytes=24 * 2**20),
        cost_estimate=pl.CostEstimate(
            flops=6 * 4 * 512 * 512 * 512, bytes_accessed=10 * 2**20, transcendentals=0
        ),
        name="gradients",
    )(core, own, other, mine, theirs, first, got, loss)


def spread_scales(scales):
    terms = []
    for _ in range(3):
        term = scales.astype(bf16)
        terms.append(term.astype(f32))
        scales = scales - terms[-1]
    left = jnp.concatenate(terms + [jnp.zeros((2, scales.shape[1]), f32)], 0).astype(bf16)
    place = lax.broadcasted_iota(jnp.int32, (8, 512), 0) % 2
    block = lax.broadcasted_iota(jnp.int32, (8, 512), 1) // BLOCK
    return contract_first(left, jnp.where(place == block, 1.0, 0.0).astype(bf16))


def adam_kernel(
    shared, weight, grad, first, second, first_scale, second_scale,
    new_weight, new_first, new_second, new_first_scale, new_second_scale, loss,
):
    rows = weight.shape[1]
    total = jnp.sum(shared[:, 0, :], 0, keepdims=True)
    loss[...] = total[:, 1:2]
    clip = jnp.minimum(1.0, clip_norm / (jnp.sqrt(total[:, 0:1]) + 1e-06))
    tap = pl.program_id(0)
    here = pl.ds(pl.multiple_of(pl.program_id(1) * rows, rows), rows)
    old_first = spread_scales(first_scale[tap, :, here] * beta_first)
    old_second = spread_scales(second_scale[tap, :, here] * beta_second)
    new_columns = []
    for block in range(2):
        span = slice(block * BLOCK, (block + 1) * BLOCK)
        clipped = grad[0, :, span] * clip
        first_new = (
            first[0, :, span].astype(f32) * old_first[:, span]
            + (1.0 - beta_first) * clipped
        )
        second_new = (
            second[0, :, span].astype(f32) * old_second[:, span]
            + (1.0 - beta_second) * clipped * clipped
        )
        current = weight[0, :, span].astype(f32)
        spread_sq = second_new * (1.0 / (1.0 - beta_second**step_count))
        spread = spread_sq * lax.rsqrt(spread_sq) + adam_eps
        turned = pl.reciprocal(spread, approx=True)
        turned = turned * (2.0 - spread * turned)
        step = first_new * turned * (learn_rate / (1.0 - beta_first**step_count))
        new_weight[0, :, span] = (
            current * (1.0 - learn_rate * weight_decay) - step
        ).astype(bf16)
        first_top = jnp.max(jnp.abs(first_new), -1, keepdims=True) + scale_eps
        second_top = jnp.max(jnp.abs(second_new), -1, keepdims=True) + scale_eps
        new_first[0, :, span] = (first_new * (1.0 / first_top)).astype(bf16)
        new_second[0, :, span] = (second_new * (1.0 / second_top)).astype(bf16)
        new_columns.append((first_top, second_top))
    lane = lax.broadcasted_iota(jnp.int32, (rows, LANES), 1)
    table = jnp.zeros((rows, LANES), f32)
    for block, (first_top, second_top) in enumerate(new_columns):
        table = jnp.where(lane == block, first_top, table)
        table = jnp.where(lane == 2 + block, second_top, table)
    turned = table.T
    new_first_scale[tap, :, here] = turned[0:2]
    new_second_scale[tap, :, here] = turned[2:4]


def adam(shared, weight, grad, first, second, first_scale, second_scale):
    rows = 512
    wide = pl.BlockSpec((1, rows, 512), lambda s, i: (s, i, 0))
    thin = pl.BlockSpec((3, 2, 1024), lambda s, i: (0, 0, 0))
    return pl.pallas_call(
        adam_kernel,
        grid=(3, 1024 // rows),
        in_specs=[
            pl.BlockSpec((128, 1, LANES), lambda s, i: (0, 0, 0)),
            wide, wide, wide, wide, thin, thin,
        ],
        out_specs=[
            wide, wide, wide, thin, thin, pl.BlockSpec((1, 1), lambda s, i: (0, 0))
        ],
        out_shape=[
            jax.ShapeDtypeStruct((3, 1024, 512), bf16),
            jax.ShapeDtypeStruct((3, 1024, 512), bf16),
            jax.ShapeDtypeStruct((3, 1024, 512), bf16),
            jax.ShapeDtypeStruct((3, 2, 1024), f32),
            jax.ShapeDtypeStruct((3, 2, 1024), f32),
            jax.ShapeDtypeStruct((1, 1), f32),
        ],
        compiler_params=pltpu.CompilerParams(vmem_limit_bytes=34 * 2**20),
        name="update",
    )(shared, weight, grad, first, second, first_scale, second_scale)


def shards(
    taps, gain, join_weight, head_weight, targets, masks,
    first_codes, first_scales, second_codes, second_scales,
):
    core = lax.axis_index("b")
    row = lax.axis_index("p")
    column = lax.axis_index("m")
    own = core.reshape(1).astype(jnp.int32)
    other = 1 - own
    group = (2 * row + core).reshape(1).astype(jnp.int32)
    chips = ("p", "m")

    def swap(value):
        return lax.ppermute(value, "b", [(0, 1), (1, 0)])

    def exchange(value, axes=chips):
        return lax.all_to_all(value, axes, 0, 0, tiled=False)

    target_ids = jnp.swapaxes(targets, 1, 2)
    mask_ids = jnp.swapaxes(masks, 1, 2)
    gain_rows = gain.reshape(4, LANES)
    gain_high = lax.reduce_precision(gain_rows, 8, 7)
    live = jnp.sum(masks.astype(f32), axis=(1, 2)).reshape(1, STEPS)
    side = jnp.concatenate(
        [
            jnp.where(column % 2 == 0, gain_high, gain_rows - gain_high),
            jnp.pad(live, ((0, 3), (0, LANES - STEPS))),
        ]
    )
    rows_f32, table = ((CHUNKS, 8, 512), f32), ((8, LANES), f32)
    vocab_f32 = ((CHUNKS, 8, 1024), f32)
    blocks = ((64, 8, 512), bf16)
    half_flops = 2 * 512**3

    with jax.named_scope("taps_in"):
        kept, outgoing = call(
            half_out_kernel, "half_out", [((3, 4, D // 2), bf16)] * 2,
            ("s", group), ("v", taps),
        )
        packed = call(
            half_join_kernel, "half_join", [((64, 24, 512), bf16)],
            ("s", own), ("v", kept), ("v", swap(outgoing)),
        )
        landed = exchange(packed)
        taps_own = landed.reshape(64, 3, 8, 512).transpose(1, 0, 2, 3).reshape(3, 512, 512)
        taps_other = swap(taps_own)

    with jax.named_scope("join_first"):
        begun = call(
            join_own_kernel, "join_own", [((2, 512, 512), f32)],
            ("s", own), ("v", taps_own), ("v", join_weight),
            flops=3 * half_flops,
        )
        constant, parts = call(
            join_other_kernel, "join_other",
            [((512, 512), f32), ((64, 8, 640), bf16)],
            ("s", other), ("v", taps_other), ("v", join_weight), ("v", begun), ("v", side),
            flops=3 * half_flops,
        )
        joining_first, gains, counts, squares = call(
            first_rows_kernel, "first_rows", [rows_f32, rows_f32, table, table],
            ("v", exchange(parts)),
        )

    def to_hidden(joining, squares):
        inverse, copies = call(
            norm_kernel, "norm", [table, blocks],
            ("v", joining), ("v", gains), ("v", squares), ("v", swap(squares)),
        )
        mine = exchange(copies).reshape(512, 512)
        return inverse, mine, swap(mine)

    with jax.named_scope("hidden_first"):
        inverse_first, hidden_mine, hidden_theirs = to_hidden(joining_first, squares)

    with jax.named_scope("join_second"):
        parts = call(
            join_second_kernel, "join_second", [((64, 8, 1536), bf16)],
            ("s", own), ("v", hidden_mine), ("v", hidden_theirs), ("v", join_weight),
            ("v", head_weight), ("v", constant),
            flops=6 * half_flops,
        )
        joining_second, logits_first, squares = call(
            second_rows_kernel, "second_rows", [rows_f32, vocab_f32, table],
            ("v", exchange(parts)),
        )

    with jax.named_scope("hidden_second"):
        inverse_second, later_mine, later_theirs = to_hidden(joining_second, squares)

    with jax.named_scope("logits"):
        parts = call(
            logits_kernel, "logits", [((64, 8, 1024), bf16)],
            ("s", own), ("v", later_mine), ("v", later_theirs), ("v", head_weight),
            flops=4 * half_flops,
        )
        got = exchange(parts)

    with jax.named_scope("softmax"):
        logits_second, stats = call(
            stats_kernel, "stats", [vocab_f32, table],
            ("s", group), ("v", got), ("v", logits_first), ("v", target_ids),
        )
        grads_first, copies, loss = call(
            logit_grad_kernel, "logit_grad",
            [((CHUNKS, 8, 1024), bf16), ((64, 8, 1024), bf16), table],
            ("s", group), ("v", stats), ("v", swap(stats)), ("v", logits_first),
            ("v", logits_second), ("v", target_ids), ("v", mask_ids), ("v", counts),
            specs=[
                whole_block((8, LANES)), whole_block((8, LANES)),
                whole_block((CHUNKS, 8, 1024)), whole_block((CHUNKS, 8, 1024)),
                whole_block((STEPS, 4, 16)), whole_block((STEPS, 4, 16)),
                whole_block((8, LANES)),
            ],
        )
        grads_second = exchange(copies).reshape(512, 1024)

    def row_gradients(parts, joining, inverse, *riders):
        scaled, inner = call(
            norm_inner_kernel, "norm_inner", [rows_f32, table],
            ("v", exchange(parts)), ("v", joining), ("v", gains),
        )
        width = 512 + sum(rider.shape[-1] for rider in riders)
        copies = call(
            norm_back_kernel, "norm_back", [((64, 8, width), bf16)],
            ("v", scaled), ("v", joining), ("v", inverse), ("v", inner),
            ("v", swap(inner)), *[("v", rider) for rider in riders],
        )
        return exchange(copies).reshape(512, width)

    with jax.named_scope("back_second"):
        operands = (("v", grads_second), ("v", head_weight))
        away = call(
            head_back_kernel, "head_away", [blocks], ("s", other), *operands,
            flops=2 * half_flops,
        )
        parts = call(
            head_back_kernel, "head_keep", [blocks], ("s", own), *operands,
            ("v", swap(away)), flops=2 * half_flops,
        )
        got = row_gradients(parts, joining_second, inverse_second, grads_first)

    with jax.named_scope("back_first"):
        operands = (("v", got), ("v", join_weight), ("v", head_weight))
        away = call(
            feed_back_kernel, "feed_away", [blocks], ("s", other), *operands,
            flops=3 * half_flops,
        )
        parts = call(
            feed_back_kernel, "feed_keep", [blocks], ("s", own), *operands,
            ("v", swap(away)), flops=3 * half_flops,
        )
        first_all = row_gradients(parts, joining_first, inverse_first)

    with jax.named_scope("gradients"):
        grads, payload = gradients(
            own, taps_own, taps_other, hidden_mine, hidden_theirs, first_all, got, loss
        )
        shared = exchange(payload, AXES)

    with jax.named_scope("update"):
        new_join, new_first, new_second, first_scale, second_scale, loss = adam(
            shared,
            join_weight,
            grads,
            first_codes,
            second_codes,
            jnp.swapaxes(first_scales, 1, 2),
            jnp.swapaxes(second_scales, 1, 2),
        )
    return (
        new_join,
        new_first,
        jnp.swapaxes(first_scale, 1, 2),
        new_second,
        jnp.swapaxes(second_scale, 1, 2),
        loss.reshape(()),
    )


def solution(mesh):
    rows = mesh.shape["dp"] // 2
    fine = Mesh(mesh.devices.reshape(rows, 2, mesh.shape["mp"]), AXES)
    dp, mp = ("p", "b"), "m"
    return jax.shard_map(
        shards,
        mesh=fine,
        in_specs=(
            P(None, ("p", "b", "m"), None),
            P(dp),
            P(None, mp, dp),
            P(mp, dp),
            P(None, None, mp),
            P(None, None, mp),
            P(None, mp, dp),
            P(None, mp, dp),
            P(None, mp, dp),
            P(None, mp, dp),
        ),
        out_specs=(
            P(None, mp, dp),
            P(None, mp, dp),
            P(None, mp, dp),
            P(None, mp, dp),
            P(None, mp, dp),
            P(),
        ),
        check_vma=False,
    )
```

```python
import jax
import jax.numpy as jnp
from jax import lax
from jax.experimental import pallas as pl
from jax.experimental.pallas import tpu as pltpu
from jax.sharding import Mesh, PartitionSpec as P

D = 8192
STEPS = 2
BLOCK = 256
LANES = 128
CHUNKS = 8

norm_eps = 1e-05
clip_norm = 1.0
learn_rate = 0.0003
weight_decay = 0.1
beta_first = 0.9
beta_second = 0.999
step_count = 10.0
adam_eps = 1e-08
scale_eps = 1e-12

bf16 = jnp.bfloat16
f32 = jnp.float32
AXES = ("p", "b", "m")
VMEM = pl.BlockSpec(memory_space=pltpu.VMEM)
SMEM = pl.BlockSpec(memory_space=pltpu.SMEM)


def dot(left, right):
    return jnp.dot(left, right, preferred_element_type=f32)


def contract_last(left, right):
    return lax.dot_general(
        left, right, (((1,), (1,)), ((), ())), preferred_element_type=f32
    )


def contract_first(left, right):
    return lax.dot_general(
        left, right, (((0,), (0,)), ((), ())), preferred_element_type=f32
    )


def put_lanes(rows, columns):
    lane = lax.broadcasted_iota(jnp.int32, (rows, LANES), 1)
    block = jnp.zeros((rows, LANES), f32)
    for place, column in enumerate(columns):
        block = jnp.where(lane == place, column, block)
    return block


def total_over(parts, picks, start, stop):
    total = parts[picks[0], :, start:stop].astype(f32)
    for pick in picks[1:]:
        total += parts[pick, :, start:stop].astype(f32)
    return total


def column_sum(parts, row, start, stop):
    return total_over(parts, [row * CHUNKS + m for m in range(CHUNKS)], start, stop)


def row_sum(parts, column, start, stop):
    return total_over(parts, [p * CHUNKS + column for p in range(CHUNKS)], start, stop)


def lane_total(values):
    total = values[0]
    for value in values[1:]:
        total = total + value
    return jnp.broadcast_to(jnp.sum(total, -1, keepdims=True), (8, LANES))


def to_blocks(value):
    return value.reshape(64, 8, value.shape[-1]).astype(bf16)


def half_rows(core):
    return pl.ds(pl.multiple_of(core * 512, 512), 512)


def call(kernel, name, outs, *operands, specs=None, flops=0):
    options = {}
    if specs is None:
        options["in_specs"] = [SMEM if space == "s" else VMEM for space, _ in operands]
        options["out_specs"] = [VMEM] * len(outs)
    else:
        options["grid_spec"] = pltpu.PrefetchScalarGridSpec(
            num_scalar_prefetch=1,
            grid=(1,),
            in_specs=specs,
            out_specs=[whole_block(shape) for shape, _ in outs],
        )
    result = pl.pallas_call(
        kernel,
        out_shape=[jax.ShapeDtypeStruct(shape, dtype) for shape, dtype in outs],
        compiler_params=pltpu.CompilerParams(vmem_limit_bytes=24 * 2**20),
        cost_estimate=pl.CostEstimate(
            flops=flops, bytes_accessed=4 * 2**20, transcendentals=0
        ),
        name=name,
        **options,
    )(*[operand for _, operand in operands])
    return result[0] if len(outs) == 1 else result


def whole_block(shape):
    return pl.BlockSpec(shape, lambda i, core: (0,) * len(shape))


def half_out_kernel(group, taps, kept, out):
    sets, _, width = taps.shape
    core = group[0] % 2
    for s in range(sets):
        for chunk in range(width // 1024):
            place = slice(chunk * 512, (chunk + 1) * 512)
            for half, target in ((core, kept), (1 - core, out)):
                start = pl.multiple_of(chunk * 1024 + half * 512, 512)
                target[s, :, place] = taps[s, :, pl.ds(start, 512)]


def half_join_kernel(core, kept, received, out):
    sets, _, width = kept.shape
    chunks = width // 512
    copies = out.shape[0] // chunks
    first = core[0] == 0
    for chunk in range(chunks):
        rows = []
        for s in range(sets):
            mine = kept[s, :, chunk * 512 : (chunk + 1) * 512].astype(f32)
            theirs = received[s, :, chunk * 512 : (chunk + 1) * 512].astype(f32)
            rows.append(jnp.where(first, mine, theirs))
            rows.append(jnp.where(first, theirs, mine))
        block = jnp.concatenate(rows, axis=0).astype(bf16)
        for copy in range(copies):
            out[copy * chunks + chunk] = block


def join_own_kernel(core, taps, weight, out):
    rows = half_rows(core[0])
    out[0] = dot(taps[0], weight[0, rows]) + dot(taps[1], weight[1, rows])
    out[1] = dot(taps[2], weight[2, rows])


def join_other_kernel(core, taps, weight, begun, side, constant, out):
    rows = half_rows(core[0])
    fixed = begun[0] + dot(taps[0], weight[0, rows]) + dot(taps[1], weight[1, rows])
    constant[...] = fixed
    out[:, :, :512] = to_blocks(fixed + begun[1] + dot(taps[2], weight[2, rows]))
    out[:, :, 512:] = jnp.broadcast_to(side[...], (64, 8, LANES)).astype(bf16)


def both_halves(core, mine, theirs, weight):
    return dot(mine[...], weight[half_rows(core[0])]) + dot(
        theirs[...], weight[half_rows(1 - core[0])]
    )


def join_second_kernel(core, mine, theirs, weight, head, constant, out):
    joined = constant[...] + both_halves(core, mine, theirs, weight.at[2])
    out[:, :, :512] = to_blocks(joined)
    out[:, :, 512:] = to_blocks(both_halves(core, mine, theirs, head))


def logits_kernel(core, mine, theirs, head, out):
    out[...] = to_blocks(both_halves(core, mine, theirs, head))


def head_back_kernel(core, grads, head, *rest):
    *added, out = rest
    value = contract_last(grads[...], head[half_rows(core[0])])
    if added:
        value += added[0][...].astype(f32).reshape(512, 512)
    out[...] = to_blocks(value)


def feed_back_kernel(core, got, weight, head, *rest):
    *added, out = rest
    rows = half_rows(core[0])
    value = contract_last(got[:, :512], weight[2, rows])
    value += contract_last(got[:, 512:], head[rows])
    if added:
        value += added[0][...].astype(f32).reshape(512, 512)
    out[...] = to_blocks(value)


def first_rows_kernel(got, joining, gain, counts, squares):
    terms = []
    for chunk in range(CHUNKS):
        value = column_sum(got, chunk, 0, 512)
        joining[chunk] = value
        terms.append(value * value)
        side = total_over(got, [chunk * CHUNKS, chunk * CHUNKS + 1], 512, 640)
        row = jnp.concatenate([side[i : i + 1] for i in range(4)], axis=1)
        gain[chunk] = jnp.broadcast_to(row, (8, 512))
    squares[...] = lane_total(terms)
    counts[...] = jnp.broadcast_to(column_sum(got, 0, 512, 640)[4:5], (8, LANES))


def second_rows_kernel(got, joining, logits, squares):
    terms = []
    for chunk in range(CHUNKS):
        value = column_sum(got, chunk, 0, 512)
        joining[chunk] = value
        terms.append(value * value)
        logits[chunk] = column_sum(got, chunk, 512, 1536)
    squares[...] = lane_total(terms)


def norm_kernel(joining, gain, squares, squares_other, inverse, out):
    factor = lax.rsqrt((squares[...] + squares_other[...]) / D + norm_eps)
    inverse[...] = factor
    for chunk in range(CHUNKS):
        hidden = (joining[chunk] * factor[:, 0:1] * gain[chunk]).astype(bf16)
        for copy in range(CHUNKS):
            out[copy * CHUNKS + chunk] = hidden


def norm_inner_kernel(got, joining, gain, scaled, inner):
    terms = []
    for chunk in range(CHUNKS):
        value = row_sum(got, chunk, 0, 512) * gain[chunk]
        scaled[chunk] = value
        terms.append(value * joining[chunk])
    inner[...] = lane_total(terms)


def norm_back_kernel(scaled, joining, inverse, inner, inner_other, *rest):
    *riders, out = rest
    factor = inverse[:, 0:1]
    pull = factor * factor * factor * (inner[:, 0:1] + inner_other[:, 0:1]) / D
    for chunk in range(CHUNKS):
        grad = (factor * scaled[chunk] - pull * joining[chunk]).astype(bf16)
        for copy in range(CHUNKS):
            out[chunk * CHUNKS + copy, :, :512] = grad
            if riders:
                out[chunk * CHUNKS + copy, :, 512:] = riders[0][chunk]


def vocab_of(core, chunk):
    return lax.broadcasted_iota(jnp.int32, (8, 1024), 1) + (2 * chunk + core) * 1024


def own_tokens(group, values):
    wide = values.astype(f32)
    lane = lax.broadcasted_iota(jnp.int32, wide.shape, 1)
    return jnp.concatenate(
        [
            jnp.sum(jnp.where(lane == group[0] - group[0] % 2 + i, wide, 0.0), -1, keepdims=True)
            for i in range(2)
        ],
        axis=0,
    )


def stats_kernel(group, got, logits_first, targets, logits_second, stats):
    for chunk in range(CHUNKS):
        logits_second[chunk] = column_sum(got, chunk, 0, 1024)
    columns = []
    for step, logits in enumerate((logits_first, logits_second)):
        top = logits[0]
        for chunk in range(1, CHUNKS):
            top = jnp.maximum(top, logits[chunk])
        top = jnp.max(top, -1, keepdims=True)
        weights = jnp.zeros((8, 1024), f32)
        target = own_tokens(group, targets[step]).astype(jnp.int32)
        picked = jnp.zeros((8, 1024), f32)
        for chunk in range(CHUNKS):
            weights += jnp.exp(logits[chunk] - top)
            hit = vocab_of(group[0] % 2, chunk) == target
            picked += jnp.where(hit, logits[chunk], 0.0)
        columns += [
            top,
            jnp.sum(weights, -1, keepdims=True),
            jnp.sum(picked, -1, keepdims=True),
        ]
    stats[...] = put_lanes(8, columns)


def logit_grad_kernel(
    group, stats, stats_other, logits_first, logits_second, targets, masks, counts,
    grads_first, grads_second, loss,
):
    lost = jnp.zeros((8, 1), f32)
    for step, logits in enumerate((logits_first, logits_second)):
        place = 3 * step
        top_mine, top_other = [x[:, place : place + 1] for x in (stats, stats_other)]
        sum_mine, sum_other = [
            x[:, place + 1 : place + 2] for x in (stats, stats_other)
        ]
        picked = stats[:, place + 2 : place + 3] + stats_other[:, place + 2 : place + 3]
        top = jnp.maximum(top_mine, top_other)
        total = sum_mine * jnp.exp(top_mine - top) + sum_other * jnp.exp(top_other - top)
        log_total = top + jnp.log(total)
        weight = own_tokens(group, masks[step]) / counts[:, step : step + 1]
        target = own_tokens(group, targets[step]).astype(jnp.int32)
        lost += weight * (log_total - picked)
        for chunk in range(CHUNKS):
            probs = jnp.exp(logits[chunk] - log_total)
            hit = jnp.where(vocab_of(group[0] % 2, chunk) == target, 1.0, 0.0)
            grad = (weight * (probs - hit)).astype(bf16)
            if step == 0:
                grads_first[chunk] = grad
            else:
                for copy in range(CHUNKS):
                    grads_second[chunk * CHUNKS + copy] = grad
    once = jnp.where(group[0] % 2 == 0, 1.0, 0.0)
    loss[...] = jnp.broadcast_to(jnp.sum(lost, 0, keepdims=True) * once, (8, LANES))


def grad_kernel(
    core, own, other, mine, theirs, first, second, loss, grad, payload, squares, summed
):
    tap = pl.program_id(0)

    def both(values):
        for half, value in enumerate(values):
            grad[0, half_rows(core[0] if half == 0 else 1 - core[0])] = value
            total = jnp.sum((value * value).reshape(-1, 8, 512), 0)
            total = total[:, :128] + total[:, 128:256] + total[:, 256:384] + total[:, 384:]
            squares[...] += total

    @pl.when(tap == 0)
    def _():
        squares[...] = jnp.zeros((8, LANES), f32)
        summed[...] = (first[...].astype(f32) + second[...].astype(f32)).astype(bf16)

    @pl.when(tap < 2)
    def _():
        both([contract_first(left[0], summed[...]) for left in (own, other)])

    @pl.when(tap == 2)
    def _():
        both(
            [
                contract_first(left[0], first[...]) + contract_first(later[...], second[...])
                for left, later in ((own, mine), (other, theirs))
            ]
        )
        row = jnp.sum(squares[...], 0, keepdims=True)
        total = jnp.sum(row, -1, keepdims=True)
        lane = lax.broadcasted_iota(jnp.int32, (1, LANES), 1)
        value = jnp.where(lane == 0, total, loss[0:1])
        payload[...] = jnp.broadcast_to(value[None], payload.shape)


def gradients(core, own, other, mine, theirs, first, got, loss):
    tap = lambda s, core: (s, 0, 0)
    still = pl.BlockSpec((512, 512), lambda s, core: (0, 0))
    return pl.pallas_call(
        grad_kernel,
        grid_spec=pltpu.PrefetchScalarGridSpec(
            num_scalar_prefetch=1,
            grid=(3,),
            in_specs=[
                pl.BlockSpec((1, 512, 512), tap),
                pl.BlockSpec((1, 512, 512), tap),
                still,
                still,
                still,
                still,
                pl.BlockSpec((8, LANES), lambda s, core: (0, 0)),
            ],
            out_specs=[
                pl.BlockSpec((1, 1024, 512), tap),
                pl.BlockSpec((128, 1, LANES), lambda s, core: (0, 0, 0)),
            ],
            scratch_shapes=[pltpu.VMEM((8, LANES), f32), pltpu.VMEM((512, 512), bf16)],
        ),
        out_shape=[
            jax.ShapeDtypeStruct((3, 1024, 512), f32),
            jax.ShapeDtypeStruct((128, 1, LANES), f32),
        ],
        compiler_params=pltpu.CompilerParams(vmem_limit_bytes=24 * 2**20),
        cost_estimate=pl.CostEstimate(
            flops=6 * 4 * 512 * 512 * 512, bytes_accessed=10 * 2**20, transcendentals=0
        ),
        name="gradients",
    )(core, own, other, mine, theirs, first, got, loss)


def spread_scales(scales):
    terms = []
    for _ in range(3):
        term = scales.astype(bf16)
        terms.append(term.astype(f32))
        scales = scales - terms[-1]
    left = jnp.concatenate(terms + [jnp.zeros((2, scales.shape[1]), f32)], 0).astype(bf16)
    place = lax.broadcasted_iota(jnp.int32, (8, 512), 0) % 2
    block = lax.broadcasted_iota(jnp.int32, (8, 512), 1) // BLOCK
    return contract_first(left, jnp.where(place == block, 1.0, 0.0).astype(bf16))


def adam_kernel(
    shared, weight, grad, first, second, first_scale, second_scale,
    new_weight, new_first, new_second, new_first_scale, new_second_scale, loss,
):
    rows = grad.shape[1]
    total = jnp.sum(shared[:, 0, :], 0, keepdims=True)
    loss[...] = total[:, 1:2]
    clip = jnp.minimum(1.0, clip_norm / (jnp.sqrt(total[:, 0:1]) + 1e-06))
    tap = pl.program_id(0)
    here = pl.ds(pl.multiple_of(pl.program_id(1) * rows, rows), rows)
    old_first = spread_scales(first_scale[tap, :, here] * beta_first)
    old_second = spread_scales(second_scale[tap, :, here] * beta_second)
    new_columns = []
    for block in range(2):
        span = slice(block * BLOCK, (block + 1) * BLOCK)
        clipped = grad[0, :, span] * clip
        first_new = (
            first[tap, here, span].astype(f32) * old_first[:, span]
            + (1.0 - beta_first) * clipped
        )
        second_new = (
            second[tap, here, span].astype(f32) * old_second[:, span]
            + (1.0 - beta_second) * clipped * clipped
        )
        current = weight[tap, here, span].astype(f32)
        spread_sq = second_new * (1.0 / (1.0 - beta_second**step_count))
        spread = spread_sq * lax.rsqrt(spread_sq) + adam_eps
        turned = pl.reciprocal(spread, approx=True)
        turned = turned * (2.0 - spread * turned)
        step = first_new * turned * (learn_rate / (1.0 - beta_first**step_count))
        new_weight[0, :, span] = (
            current * (1.0 - learn_rate * weight_decay) - step
        ).astype(bf16)
        first_top = jnp.max(jnp.abs(first_new), -1, keepdims=True) + scale_eps
        second_top = jnp.max(jnp.abs(second_new), -1, keepdims=True) + scale_eps
        new_first[0, :, span] = (first_new * (1.0 / first_top)).astype(bf16)
        new_second[0, :, span] = (second_new * (1.0 / second_top)).astype(bf16)
        new_columns.append((first_top, second_top))
    lane = lax.broadcasted_iota(jnp.int32, (rows, LANES), 1)
    table = jnp.zeros((rows, LANES), f32)
    for block, (first_top, second_top) in enumerate(new_columns):
        table = jnp.where(lane == block, first_top, table)
        table = jnp.where(lane == 2 + block, second_top, table)
    turned = table.T
    new_first_scale[tap, :, here] = turned[0:2]
    new_second_scale[tap, :, here] = turned[2:4]


def adam(shared, weight, grad, first, second, first_scale, second_scale):
    rows = 512
    wide = pl.BlockSpec((1, rows, 512), lambda s, i: (s, i, 0))
    thin = pl.BlockSpec((3, 2, 1024), lambda s, i: (0, 0, 0))
    return pl.pallas_call(
        adam_kernel,
        grid=(3, 1024 // rows),
        in_specs=[
            pl.BlockSpec((128, 1, LANES), lambda s, i: (0, 0, 0)),
            VMEM, wide, VMEM, VMEM, thin, thin,
        ],
        out_specs=[
            wide, wide, wide, thin, thin, pl.BlockSpec((1, 1), lambda s, i: (0, 0))
        ],
        out_shape=[
            jax.ShapeDtypeStruct((3, 1024, 512), bf16),
            jax.ShapeDtypeStruct((3, 1024, 512), bf16),
            jax.ShapeDtypeStruct((3, 1024, 512), bf16),
            jax.ShapeDtypeStruct((3, 2, 1024), f32),
            jax.ShapeDtypeStruct((3, 2, 1024), f32),
            jax.ShapeDtypeStruct((1, 1), f32),
        ],
        compiler_params=pltpu.CompilerParams(vmem_limit_bytes=34 * 2**20),
        name="update",
    )(shared, weight, grad, first, second, first_scale, second_scale)


def shards(
    taps, gain, join_weight, head_weight, targets, masks,
    first_codes, first_scales, second_codes, second_scales,
):
    core = lax.axis_index("b")
    row = lax.axis_index("p")
    column = lax.axis_index("m")
    own = core.reshape(1).astype(jnp.int32)
    other = 1 - own
    group = (2 * row + core).reshape(1).astype(jnp.int32)
    chips = ("p", "m")

    def swap(value):
        return lax.ppermute(value, "b", [(0, 1), (1, 0)])

    def exchange(value, axes=chips):
        return lax.all_to_all(value, axes, 0, 0, tiled=False)

    target_ids = jnp.swapaxes(targets, 1, 2)
    mask_ids = jnp.swapaxes(masks, 1, 2)
    gain_rows = gain.reshape(4, LANES)
    gain_high = lax.reduce_precision(gain_rows, 8, 7)
    live = jnp.sum(masks.astype(f32), axis=(1, 2)).reshape(1, STEPS)
    side = jnp.concatenate(
        [
            jnp.where(column % 2 == 0, gain_high, gain_rows - gain_high),
            jnp.pad(live, ((0, 3), (0, LANES - STEPS))),
        ]
    )
    rows_f32, table = ((CHUNKS, 8, 512), f32), ((8, LANES), f32)
    vocab_f32 = ((CHUNKS, 8, 1024), f32)
    blocks = ((64, 8, 512), bf16)
    half_flops = 2 * 512**3

    with jax.named_scope("taps_in"):
        kept, outgoing = call(
            half_out_kernel, "half_out", [((3, 4, D // 2), bf16)] * 2,
            ("s", group), ("v", taps),
        )
        packed = call(
            half_join_kernel, "half_join", [((64, 24, 512), bf16)],
            ("s", own), ("v", kept), ("v", swap(outgoing)),
        )
        landed = exchange(packed)
        taps_own = landed.reshape(64, 3, 8, 512).transpose(1, 0, 2, 3).reshape(3, 512, 512)
        taps_other = swap(taps_own)

    with jax.named_scope("join_first"):
        begun = call(
            join_own_kernel, "join_own", [((2, 512, 512), f32)],
            ("s", own), ("v", taps_own), ("v", join_weight),
            flops=3 * half_flops,
        )
        constant, parts = call(
            join_other_kernel, "join_other",
            [((512, 512), f32), ((64, 8, 640), bf16)],
            ("s", other), ("v", taps_other), ("v", join_weight), ("v", begun), ("v", side),
            flops=3 * half_flops,
        )
        joining_first, gains, counts, squares = call(
            first_rows_kernel, "first_rows", [rows_f32, rows_f32, table, table],
            ("v", exchange(parts)),
        )

    def to_hidden(joining, squares):
        inverse, copies = call(
            norm_kernel, "norm", [table, blocks],
            ("v", joining), ("v", gains), ("v", squares), ("v", swap(squares)),
        )
        mine = exchange(copies).reshape(512, 512)
        return inverse, mine, swap(mine)

    with jax.named_scope("hidden_first"):
        inverse_first, hidden_mine, hidden_theirs = to_hidden(joining_first, squares)

    with jax.named_scope("join_second"):
        parts = call(
            join_second_kernel, "join_second", [((64, 8, 1536), bf16)],
            ("s", own), ("v", hidden_mine), ("v", hidden_theirs), ("v", join_weight),
            ("v", head_weight), ("v", constant),
            flops=6 * half_flops,
        )
        joining_second, logits_first, squares = call(
            second_rows_kernel, "second_rows", [rows_f32, vocab_f32, table],
            ("v", exchange(parts)),
        )

    with jax.named_scope("hidden_second"):
        inverse_second, later_mine, later_theirs = to_hidden(joining_second, squares)

    with jax.named_scope("logits"):
        parts = call(
            logits_kernel, "logits", [((64, 8, 1024), bf16)],
            ("s", own), ("v", later_mine), ("v", later_theirs), ("v", head_weight),
            flops=4 * half_flops,
        )
        got = exchange(parts)

    with jax.named_scope("softmax"):
        logits_second, stats = call(
            stats_kernel, "stats", [vocab_f32, table],
            ("s", group), ("v", got), ("v", logits_first), ("v", target_ids),
        )
        grads_first, copies, loss = call(
            logit_grad_kernel, "logit_grad",
            [((CHUNKS, 8, 1024), bf16), ((64, 8, 1024), bf16), table],
            ("s", group), ("v", stats), ("v", swap(stats)), ("v", logits_first),
            ("v", logits_second), ("v", target_ids), ("v", mask_ids), ("v", counts),
            specs=[
                whole_block((8, LANES)), whole_block((8, LANES)),
                whole_block((CHUNKS, 8, 1024)), whole_block((CHUNKS, 8, 1024)),
                whole_block((STEPS, 4, 16)), whole_block((STEPS, 4, 16)),
                whole_block((8, LANES)),
            ],
        )
        grads_second = exchange(copies).reshape(512, 1024)

    def row_gradients(parts, joining, inverse, *riders):
        scaled, inner = call(
            norm_inner_kernel, "norm_inner", [rows_f32, table],
            ("v", exchange(parts)), ("v", joining), ("v", gains),
        )
        width = 512 + sum(rider.shape[-1] for rider in riders)
        copies = call(
            norm_back_kernel, "norm_back", [((64, 8, width), bf16)],
            ("v", scaled), ("v", joining), ("v", inverse), ("v", inner),
            ("v", swap(inner)), *[("v", rider) for rider in riders],
        )
        return exchange(copies).reshape(512, width)

    with jax.named_scope("back_second"):
        operands = (("v", grads_second), ("v", head_weight))
        away = call(
            head_back_kernel, "head_away", [blocks], ("s", other), *operands,
            flops=2 * half_flops,
        )
        parts = call(
            head_back_kernel, "head_keep", [blocks], ("s", own), *operands,
            ("v", swap(away)), flops=2 * half_flops,
        )
        got = row_gradients(parts, joining_second, inverse_second, grads_first)

    with jax.named_scope("back_first"):
        operands = (("v", got), ("v", join_weight), ("v", head_weight))
        away = call(
            feed_back_kernel, "feed_away", [blocks], ("s", other), *operands,
            flops=3 * half_flops,
        )
        parts = call(
            feed_back_kernel, "feed_keep", [blocks], ("s", own), *operands,
            ("v", swap(away)), flops=3 * half_flops,
        )
        first_all = row_gradients(parts, joining_first, inverse_first)

    with jax.named_scope("gradients"):
        grads, payload = gradients(
            own, taps_own, taps_other, hidden_mine, hidden_theirs, first_all, got, loss
        )
        shared = exchange(payload, AXES)

    with jax.named_scope("update"):
        new_join, new_first, new_second, first_scale, second_scale, loss = adam(
            shared,
            join_weight,
            grads,
            first_codes,
            second_codes,
            jnp.swapaxes(first_scales, 1, 2),
            jnp.swapaxes(second_scales, 1, 2),
        )
    return (
        new_join,
        new_first,
        jnp.swapaxes(first_scale, 1, 2),
        new_second,
        jnp.swapaxes(second_scale, 1, 2),
        loss.reshape(()),
    )


def solution(mesh):
    rows = mesh.shape["dp"] // 2
    fine = Mesh(mesh.devices.reshape(rows, 2, mesh.shape["mp"]), AXES)
    dp, mp = ("p", "b"), "m"
    return jax.shard_map(
        shards,
        mesh=fine,
        in_specs=(
            P(None, ("p", "b", "m"), None),
            P(dp),
            P(None, mp, dp),
            P(mp, dp),
            P(None, None, mp),
            P(None, None, mp),
            P(None, mp, dp),
            P(None, mp, dp),
            P(None, mp, dp),
            P(None, mp, dp),
        ),
        out_specs=(
            P(None, mp, dp),
            P(None, mp, dp),
            P(None, mp, dp),
            P(None, mp, dp),
            P(None, mp, dp),
            P(),
        ),
        check_vma=False,
    )
```
